32 devices in a mesh: prow: 4 (over y, core), pcol: 8 (over z, x).
Axes of the slice: x: 2, y: 2, z: 4, core: 2. Of those that a mesh axis runs over, the one named last changes fastest.
Arguments:
- right_sides: bfloat16 [16384, 128], P(('prow', 'pcol')), may hold values from -6 to 6
- factor: bfloat16 [16, 8, 32, 4, 128, 128], P(None, 'pcol', None, 'prow'), may hold values from -0.0625 to 0.0625
- pattern: int32 [16, 8, 32, 4], P(None, 'pcol', None, 'prow'), may hold values 0 or 1
- lower_inverse: bfloat16 [16, 8, 128, 128], P(None, 'pcol'), may hold values from -0.5 to 0.5
- upper_inverse: bfloat16 [16, 8, 128, 128], P(None, 'pcol'), may hold values from -0.5 to 0.5
Outputs:
- solution: bfloat16 [16384, 128], P(('prow', 'pcol'))
The draws below stay inside these ranges and needn't reach their ends.
All inputs are finite; a program needn't handle non-finite values. No bound on the sum of `pattern` on one device may be relied on, other than what follows from the above.
Results may differ from the reference program's by a relative error of at most 0.02.
Values may be sent and summed in bfloat16 or wider, within the bound.
No kernel may reach another device: no remote copies, remote signals or barrier semaphores. Data moves between devices by JAX's collectives and lax.ppermute only.
A program may use at most 128 MiB of HBM per device.

```python
import jax
import jax.numpy as jnp
from jax import lax

S = 128
NRHS = 128
NB = 128
ROWS = 16384
N_PROW = 4
N_PCOL = 8


def set_ends(array, rng, least, top_value):
    extent = array.shape
    spot = [jax.random.randint(jax.random.fold_in(rng, axis), (), 0, extent[axis]) for axis in range(len(extent))]
    array = array.at[tuple(spot)].set(least)
    longest = extent.index(max(extent))
    spot[longest] = (spot[longest] + 1) % extent[longest]
    return array.at[tuple(spot)].set(top_value)


def block_scale(key, extent, shards, low, largest):
    gain = 1.0
    for position, parts in shards:
        heights = jax.random.uniform(jax.random.fold_in(jax.random.fold_in(key, 6), position), (parts,), jnp.float32, low / len(shards), largest / len(shards))
        gain = gain * jnp.repeat(jnp.exp(heights), extent[position] // parts).reshape((-1,) + (1,) * (len(extent) - 1 - position))
    return gain


def bell_draw(rng, shape, scale, most, split=(), kind=jnp.bfloat16):
    values = scale * jax.random.normal(rng, shape, jnp.float32)
    if split:
        values = values * block_scale(rng, shape, split, -0.22, 0.18)
    return jnp.clip(values, -most, most).astype(kind)


def setup_inputs(seed: int = 0) -> dict:
    key_list = jax.random.split(jax.random.key(seed), 6)
    right_sides = bell_draw(key_list[0], (ROWS, NRHS), 1.0, 6.0, ((0, 32),))
    factor = bell_draw(key_list[1], (NB // N_PCOL, N_PCOL, NB // N_PROW, N_PROW, S, S), (NB * S // 2) ** -0.5, 0.0625, ((1, 8), (3, 4)))
    pattern = set_ends((jax.random.randint(key_list[2], (NB // N_PCOL, N_PCOL, NB // N_PROW, N_PROW), 0, 2) < 1).astype(jnp.int32), jax.random.fold_in(key_list[2], 1), 0, 1)
    lower_inverse = bell_draw(key_list[3], (NB // N_PCOL, N_PCOL, S, S), S ** -0.5, 0.5, ((1, 8),))
    upper_inverse = bell_draw(key_list[4], (NB // N_PCOL, N_PCOL, S, S), S ** -0.5, 0.5, ((1, 8),))
    return {"right_sides": right_sides, "factor": factor, "pattern": pattern, "lower_inverse": lower_inverse, "upper_inverse": upper_inverse}


def level_index(index_vals, node_count):
    bounds = (node_count // 2, 3 * node_count // 4, 7 * node_count // 8)
    result = jnp.zeros(index_vals.shape, jnp.int32)
    for edge_val in bounds:
        result = result + (index_vals >= edge_val).astype(jnp.int32)
    return result


def level_terms(row_blocks_all, keep_mask, solved):
    solved_wide = solved.astype(jnp.float32)

    def row_term(pieces):
        row_blocks, row_keep = pieces
        masked = row_blocks.astype(jnp.float32) * row_keep[:, None, None]
        return jnp.einsum("jab,jbn->an", masked, solved_wide, precision=lax.Precision.HIGHEST)

    return lax.map(row_term, (row_blocks_all, keep_mask))


def apply_inverse(inverse_blocks, remainder):
    return jnp.einsum("iab,ibn->ian", inverse_blocks.astype(jnp.float32), remainder.astype(jnp.float32), precision=lax.Precision.HIGHEST).astype(jnp.bfloat16)


def reference(right_sides, factor, pattern, lower_inverse, upper_inverse):
    node_count = NB
    blocks = factor.reshape(node_count, node_count, S, S)
    pattern_mat = pattern.reshape(node_count, node_count)
    lower_mats = lower_inverse.reshape(node_count, S, S)
    upper_mats = upper_inverse.reshape(node_count, S, S)
    right_blocks = right_sides.reshape(node_count, S, NRHS)
    levels = level_index(jnp.arange(node_count, dtype=jnp.int32), node_count)
    bounds = (0, node_count // 2, 3 * node_count // 4, 7 * node_count // 8, node_count)
    forward_vals = jnp.zeros((node_count, S, NRHS), jnp.bfloat16)
    for level_id in range(4):
        row_start, row_end = bounds[level_id], bounds[level_id + 1]
        keep_mask = ((pattern_mat[row_start:row_end] > 0) & (levels[None, :] < level_id)).astype(jnp.float32)
        summed = level_terms(blocks[row_start:row_end], keep_mask, forward_vals)
        remainder = (right_blocks[row_start:row_end].astype(jnp.float32) - summed).astype(jnp.bfloat16)
        remainder = lax.optimization_barrier(remainder)
        solved = apply_inverse(lower_mats[row_start:row_end], remainder)
        forward_vals = forward_vals.at[row_start:row_end].set(solved)
    backward_vals = jnp.zeros((node_count, S, NRHS), jnp.bfloat16)
    for level_id in (3, 2, 1, 0):
        row_start, row_end = bounds[level_id], bounds[level_id + 1]
        keep_mask = ((pattern_mat[row_start:row_end] > 0) & (levels[None, :] > level_id)).astype(jnp.float32)
        summed = level_terms(blocks[row_start:row_end], keep_mask, backward_vals)
        remainder = (forward_vals[row_start:row_end].astype(jnp.float32) - summed).astype(jnp.bfloat16)
        remainder = lax.optimization_barrier(remainder)
        solved = apply_inverse(upper_mats[row_start:row_end], remainder)
        backward_vals = backward_vals.at[row_start:row_end].set(solved)
    return backward_vals.reshape(node_count * S, NRHS)
```

```python
import functools

import jax
import jax.numpy as jnp
from jax import lax
from jax.experimental import pallas as pl
from jax.experimental.pallas import tpu as pltpu
from jax.sharding import Mesh
from jax.sharding import PartitionSpec as P

ROW_AXES = ("hi", "lo")
COL_AXES = ("q", "s")
ALL_AXES = ROW_AXES + COL_AXES
VMEM_LIMIT = 40 * 1024 * 1024


def params():
    return pltpu.CompilerParams(vmem_limit_bytes=VMEM_LIMIT)


def block_sums(scalars, pattern, factor, pieces, row_start, row_count, col_start, col_count, acc, base, negate):
    size = factor.shape[-1]
    rhs = pieces[0][0].shape[-1]
    piece_count = len(pieces)

    def first_row(scal):
        return row_start if isinstance(row_start, int) else scal[row_start[0]]

    def kernel(scal, pat, factor_ref, *refs):
        piece_refs = refs[:piece_count]
        rest = list(refs[piece_count:])
        acc_ref = rest.pop(0) if acc is not None else None
        base_ref = rest.pop(0) if base is not None else None
        out_ref = rest.pop(0)
        row = first_row(scal) + pl.program_id(0)
        total = acc_ref[0] if acc is not None else jnp.zeros((size, rhs), jnp.float32)
        for (_, pairs), ref in zip(pieces, piece_refs):
            for start, columns in pairs(scal):
                tiles = []
                for column in columns:
                    tile = factor_ref[0, 0, column - col_start, 0]
                    tiles.append(jnp.where(pat[row, column] > 0, tile, jnp.zeros_like(tile)))
                left = jnp.concatenate(tiles, axis=1)
                right = ref[start : start + len(columns)].reshape(len(columns) * size, rhs)
                total = total + jnp.dot(left, right, preferred_element_type=jnp.float32)
        if negate:
            total = -total if base is None else base_ref[0].astype(jnp.float32) - total
        out_ref[0] = total.astype(out_ref.dtype)

    in_specs = [
        pl.BlockSpec(
            (1, 1, col_count, 1, size, size),
            lambda g, scal, pat: (first_row(scal) + g, 0, col_start // col_count, 0, 0, 0),
        )
    ]
    operands = [factor]
    for blocks, _ in pieces:
        in_specs.append(pl.BlockSpec(blocks.shape, lambda g, scal, pat: (0, 0, 0)))
        operands.append(blocks)
    for extra in (acc, base):
        if extra is not None:
            array, offset = extra
            if isinstance(offset, int):
                index = lambda g, scal, pat, offset=offset: (g + offset, 0, 0)
            else:
                index = lambda g, scal, pat, offset=offset: (g + scal[offset[0]], 0, 0)
            in_specs.append(pl.BlockSpec((1, size, rhs), index))
            operands.append(array)
    out_dtype = jnp.bfloat16 if negate else jnp.float32
    return pl.pallas_call(
        kernel,
        grid_spec=pltpu.PrefetchScalarGridSpec(
            num_scalar_prefetch=2,
            grid=(row_count,),
            in_specs=in_specs,
            out_specs=pl.BlockSpec((1, size, rhs), lambda g, scal, pat: (g, 0, 0)),
        ),
        out_shape=jax.ShapeDtypeStruct((row_count, size, rhs), out_dtype),
        compiler_params=params(),
        cost_estimate=pl.CostEstimate(
            flops=2 * row_count * col_count * size * size * rhs,
            bytes_accessed=2 * row_count * col_count * size * size,
            transcendentals=0,
        ),
        name="block_sums",
    )(scalars, pattern, *operands)


def sum_and_solve(gathered, base, inverses, row_start):
    parts, rows, size, rhs = gathered.shape

    def kernel(gathered_ref, *refs):
        refs = list(refs)
        base_ref = refs.pop(0) if base is not None else None
        out_ref = refs.pop()
        for i in range(rows):
            value = gathered_ref[0, i].astype(jnp.float32)
            for part in range(1, parts):
                value = value + gathered_ref[part, i].astype(jnp.float32)
            if base is not None:
                value = value + base_ref[i].astype(jnp.float32)
            value = value.astype(jnp.bfloat16)
            for inverse_ref in refs:
                value = jnp.dot(inverse_ref[i, 0], value, preferred_element_type=jnp.float32).astype(jnp.bfloat16)
            out_ref[i] = value

    operands = [gathered]
    in_specs = [pl.BlockSpec(gathered.shape, lambda g: (0, 0, 0, 0))]
    if base is not None:
        operands.append(base)
        in_specs.append(pl.BlockSpec(base.shape, lambda g: (0, 0, 0)))
    for inverse in inverses:
        operands.append(inverse)
        in_specs.append(pl.BlockSpec((rows, 1, size, size), lambda g: (row_start // rows, 0, 0, 0)))
    return pl.pallas_call(
        kernel,
        grid=(1,),
        in_specs=in_specs,
        out_specs=pl.BlockSpec((rows, size, rhs), lambda g: (0, 0, 0)),
        out_shape=jax.ShapeDtypeStruct((rows, size, rhs), jnp.bfloat16),
        compiler_params=params(),
        cost_estimate=pl.CostEstimate(
            flops=2 * rows * size * size * rhs, bytes_accessed=2 * (parts + 2) * rows * size * rhs, transcendentals=0
        ),
        name="sum_and_solve",
    )(*operands)


def solve_copies(inverse, values, copies):
    count, size, rhs = values.shape

    def kernel(inverse_ref, value_ref, out_ref):
        for i in range(count):
            solved = jnp.dot(inverse_ref[i], value_ref[i], preferred_element_type=jnp.float32).astype(jnp.bfloat16)
            for copy in range(copies):
                out_ref[copy, i] = solved

    return pl.pallas_call(
        kernel,
        grid=(1,),
        in_specs=[
            pl.BlockSpec((count, size, size), lambda g: (0, 0, 0)),
            pl.BlockSpec((count, size, rhs), lambda g: (0, 0, 0)),
        ],
        out_specs=pl.BlockSpec((copies, count, size, rhs), lambda g: (0, 0, 0, 0)),
        out_shape=jax.ShapeDtypeStruct((copies, count, size, rhs), jnp.bfloat16),
        compiler_params=params(),
        name="solve_copies",
    )(inverse, values)


def last_solve(scalars, start_index, own, other, inverse, solved, copies):
    count, size, rhs = own.shape

    def kernel(scal, own_ref, other_ref, inverse_ref, solved_ref, out_ref):
        for h in range(count):
            value = (own_ref[h] + other_ref[h].astype(jnp.float32)).astype(jnp.bfloat16)
            value = jnp.dot(inverse_ref[h, 0], value, preferred_element_type=jnp.float32).astype(jnp.bfloat16)
            value = jnp.where(scal[start_index + 1] > 0, value, solved_ref[h])
            for copy in range(copies):
                out_ref[h * copies + copy] = value

    full = lambda g, scal: (0, 0, 0)
    return pl.pallas_call(
        kernel,
        grid_spec=pltpu.PrefetchScalarGridSpec(
            num_scalar_prefetch=1,
            grid=(1,),
            in_specs=[
                pl.BlockSpec(own.shape, full),
                pl.BlockSpec(other.shape, full),
                pl.BlockSpec((count, 1, size, size), lambda g, scal: (scal[start_index], 0, 0, 0)),
                pl.BlockSpec((count, size, rhs), lambda g, scal: (scal[start_index + 2], 0, 0)),
            ],
            out_specs=pl.BlockSpec((count * copies, size, rhs), full),
        ),
        out_shape=jax.ShapeDtypeStruct((count * copies, size, rhs), jnp.bfloat16),
        compiler_params=params(),
        name="last_solve",
    )(scalars, own, other, inverse, solved)


def on_device(right_sides, factor, pattern, lower_inverse, upper_inverse):
    lo_n = lax.axis_size("lo")
    prow_n = lax.axis_size("hi") * lo_n
    q_n = lax.axis_size("q")
    pcol_n = q_n * lax.axis_size("s")
    row_id = lax.axis_index("hi") * lo_n + lax.axis_index("lo")
    q_id = lax.axis_index("q")
    s_id = lax.axis_index("s")
    col_id = q_id * prow_n + s_id
    row_blocks, _, col_blocks, _, size, _ = factor.shape
    rhs = right_sides.shape[1]
    per = right_sides.shape[0] // size
    spread_n = pcol_n // per
    half = row_blocks // 2
    bounds = (0, half, 3 * row_blocks // 4, 7 * row_blocks // 8, row_blocks)
    cols = tuple(q_n * b for b in bounds)
    device = lambda r, c: r * pcol_n + c
    everyone = [(r, c) for r in range(prow_n) for c in range(pcol_n)]

    is_low = row_id < prow_n // 2
    lo_id = lax.axis_index("lo")
    entries = [q_id] + [per * lax.rem(lo_id + t, lo_n) for t in range(lo_n)]
    last_index = len(entries)
    entries += [lo_id, is_low.astype(jnp.int32), jnp.where(is_low, 0, lo_id)]
    scalars = jnp.stack([jnp.asarray(v, jnp.int32) for v in entries])
    pattern = pattern.reshape(row_blocks, col_blocks)
    sums = functools.partial(block_sums, scalars, pattern, factor)

    def spread(values):
        return [
            lax.ppermute(
                values,
                ALL_AXES,
                [
                    (device(r, c), device(c % prow_n, (c // prow_n + t) % q_n * prow_n + r))
                    for r, c in everyone
                ],
            )
            for t in range(q_n)
        ]

    def spread_pieces(received, first):
        result = []
        for t, blocks in enumerate(received):

            def pairs(scal, t=t, count=blocks.shape[0]):
                q = lax.rem(scal[0] + (q_n - t), q_n)
                return [(m, [q_n * (first + m + n) + q for n in range(2)]) for m in range(0, count, 2)]

            result.append((blocks, pairs))
        return result

    def gather(partial):
        return lax.all_gather(partial, ROW_AXES, axis=0)

    if per == prow_n:
        blocks = lax.all_to_all(right_sides.reshape(per, size, rhs), ROW_AXES, 0, 0, tiled=True)
        there = [(device(r, c), device(c % prow_n, r * q_n + c // prow_n)) for r, c in everyone]
        back = [(target, source) for source, target in there]
        inverse_rows = lax.dynamic_index_in_dim(
            lower_inverse[:half].reshape(half // per, per, size, size), row_id, 1, keepdims=False
        )
        inverse_rows = lax.ppermute(inverse_rows, ALL_AXES, there)
        first_half = half // per
        copies = solve_copies(inverse_rows, blocks[:first_half], pcol_n)
        zero_vals = lax.all_to_all(copies, COL_AXES, 0, 0, tiled=True)
        flat = zero_vals.reshape(pcol_n * first_half, size, rhs)

        def zero_pairs(scal):
            result = []
            for c in range(pcol_n):
                for r in range(0, first_half, 2):
                    result.append((c * first_half + r, [pcol_n * (r + n) + c for n in range(2)]))
            return result

        zero_pieces = [(flat, zero_pairs)]
        rest = lax.ppermute(blocks[first_half:], ALL_AXES, back)
        owned = (jnp.arange(per) == row_id)[None, :, None, None]
        base_rest = jnp.where(owned, rest[:, None], jnp.zeros((), jnp.bfloat16)).reshape(row_blocks - half, size, rhs)
        own_zero = lax.dynamic_index_in_dim(
            zero_vals.reshape(per, q_n, first_half, size, rhs), q_id, 1, keepdims=False
        )
        base_zero = jnp.where(row_id == s_id, jnp.swapaxes(own_zero, 0, 1), jnp.zeros((), jnp.bfloat16))
        base_zero = base_zero.reshape(half, size, rhs)
    else:
        group_rows = lax.all_gather(right_sides.reshape(per, size, rhs), COL_AXES, axis=0, tiled=True)
        picked = lax.dynamic_index_in_dim(group_rows.reshape(per, pcol_n, size, rhs), col_id, 1, keepdims=False)
        mine = lax.all_gather(picked, ROW_AXES, axis=0, tiled=True)
        zero_rows = sum_and_solve(mine[None, :half], None, [lower_inverse], 0)
        zero_pieces = spread_pieces(spread(zero_rows), 0)
        base_rest = jnp.where(row_id == 0, mine[half:], jnp.zeros((), jnp.bfloat16))
        base_zero = jnp.where(row_id == 0, zero_rows, jnp.zeros((), jnp.bfloat16))

    def count(level):
        return bounds[level + 1] - bounds[level]

    def width(first, last):
        return cols[last + 1] - cols[first]

    partial = sums(zero_pieces, bounds[1], count(1), 0, cols[1], None, (base_rest, 0), True)
    one_rows = sum_and_solve(gather(partial), None, [lower_inverse], bounds[1])
    one_pieces = spread_pieces(spread(one_rows), bounds[1])
    late = sums(zero_pieces, bounds[2], count(2) + count(3), 0, cols[1], None, None, False)
    partial = sums(
        one_pieces, bounds[2], count(2), cols[1], width(1, 1), (late, 0), (base_rest, bounds[2] - half), True
    )
    two_rows = sum_and_solve(gather(partial), None, [lower_inverse], bounds[2])
    two_pieces = spread_pieces(spread(two_rows), bounds[2])
    late = sums(one_pieces, bounds[3], count(3), cols[1], width(1, 1), (late, count(2)), None, False)
    partial = sums(
        two_pieces, bounds[3], count(3), cols[2], width(2, 2), (late, 0), (base_rest, bounds[3] - half), True
    )
    three_solved = sum_and_solve(gather(partial), None, [lower_inverse, upper_inverse], bounds[3])
    three_pieces = spread_pieces(spread(three_solved), bounds[3])
    partial = sums(three_pieces, bounds[2], count(2), cols[3], width(3, 3), None, None, True)
    two_solved = sum_and_solve(gather(partial), two_rows, [upper_inverse], bounds[2])
    two_pieces = spread_pieces(spread(two_solved), bounds[2])
    late = sums(three_pieces, bounds[1], count(1), cols[3], width(3, 3), None, None, False)
    partial = sums(two_pieces, bounds[1], count(1), cols[2], width(2, 2), (late, 0), None, True)
    one_solved = sum_and_solve(gather(partial), one_rows, [upper_inverse], bounds[1])
    one_pieces = spread_pieces(spread(one_solved), bounds[1])
    upper = sums(two_pieces + three_pieces, 0, half, cols[2], width(2, 3), None, None, False)
    chunks = []
    for t in range(1, lo_n):
        chunks.append(
            sums(one_pieces, (1 + t,), per, cols[1], width(1, 1), (upper, (1 + t,)), (base_zero, (1 + t,)), True)
        )
    own = sums(one_pieces, (1,), per, cols[1], width(1, 1), (upper, (1,)), (base_zero, (1,)), True)
    own = own.astype(jnp.float32)
    for t in range(1, lo_n):
        pairs = [((lo, (lo + t) % lo_n)) for lo in range(lo_n)]
        own = own + lax.ppermute(chunks[t - 1], "lo", pairs).astype(jnp.float32)
    other = lax.ppermute(own.astype(jnp.bfloat16), "hi", [(0, 1), (1, 0)])
    solved = jnp.concatenate([one_solved, two_solved, three_solved], axis=0)
    slots = last_solve(scalars, last_index, own, other, upper_inverse, solved, spread_n)
    received = lax.all_to_all(slots, COL_AXES, 0, 0, tiled=True)
    mine = lax.dynamic_slice_in_dim(received, lax.rem(col_id, spread_n) * per, per, 0)
    return mine.reshape(per * size, rhs)


def solution(mesh):
    prow_n, pcol_n = mesh.shape["prow"], mesh.shape["pcol"]
    fine = Mesh(mesh.devices.reshape(2, prow_n // 2, pcol_n // prow_n, prow_n), ALL_AXES)
    placed = (
        P(ALL_AXES, None),
        P(None, COL_AXES, None, ROW_AXES, None, None),
        P(None, COL_AXES, None, ROW_AXES),
        P(None, COL_AXES, None, None),
        P(None, COL_AXES, None, None),
    )
    return jax.shard_map(on_device, mesh=fine, in_specs=placed, out_specs=P(ALL_AXES, None), check_vma=False)
```

```python
import math

import jax
import jax.numpy as jnp
from jax import lax
from jax.experimental import pallas as pl
from jax.experimental.pallas import tpu as pltpu
from jax.sharding import Mesh
from jax.sharding import PartitionSpec as P

ROW_AXES = ("hi", "lo")
COL_AXES = ("q", "s")
ALL_AXES = ROW_AXES + COL_AXES
VMEM_LIMIT = 16 * 1024 * 1024


def params():
    return pltpu.CompilerParams(vmem_limit_bytes=VMEM_LIMIT)


def lay_out(scalars, pattern, factor, after, parts):
    size = factor.shape[-1]
    shapes = [(len(groups(None)), rows, 2, size, size) for rows, _, groups, _ in parts]
    copy_count = sum(len(starts(None)) * len(groups(None)) for _, starts, groups, _ in parts)
    steps = sorted({step for _, _, _, step in parts})
    operands = [factor.reshape(factor.shape[0], -1, step, size, size) for step in steps]

    def kernel(scal, pat, *refs):
        factor_refs = dict(zip(steps, refs))
        out_refs = refs[len(steps) + 1 : -1]
        sems = refs[-1]
        copies = []
        for (rows, starts, groups, step), out_ref in zip(parts, out_refs):
            run = rows // len(starts(scal))
            part_copies = []
            for g, column in enumerate(groups(scal)):
                for n, start in enumerate(starts(scal)):
                    place = sum(map(len, copies)) + len(part_copies)
                    part_copies.append(
                        pltpu.make_async_copy(
                            factor_refs[step].at[
                                pl.ds(start, run), pl.ds(column // step, 2), column % step
                            ],
                            out_ref.at[g, pl.ds(n * run, run)],
                            sems.at[place],
                        )
                    )
            for copy in part_copies:
                copy.start()
            copies.append(part_copies)
        for (rows, starts, groups, step), out_ref, part_copies in zip(parts, out_refs, copies):
            for copy in part_copies:
                copy.wait()
            first_rows = starts(scal)
            run = rows // len(first_rows)
            for n, start in enumerate(first_rows):

                def clear(i, carry, n=n, start=start):
                    for g, column in enumerate(groups(scal)):
                        for k in range(2):

                            @pl.when(pat[start + i, column + k * step] == 0)
                            def _():
                                out_ref[g, n * run + i, k] = jnp.zeros((size, size), jnp.bfloat16)

                    return carry

                lax.fori_loop(0, run, clear, 0)

    return pl.pallas_call(
        kernel,
        grid_spec=pltpu.PrefetchScalarGridSpec(
            num_scalar_prefetch=2,
            grid=(1,),
            in_specs=[pl.BlockSpec(memory_space=pl.ANY)] * (len(steps) + 1),
            out_specs=[pl.BlockSpec(memory_space=pltpu.VMEM)] * len(parts),
            scratch_shapes=[pltpu.SemaphoreType.DMA((copy_count,))],
        ),
        out_shape=[jax.ShapeDtypeStruct(shape, jnp.bfloat16) for shape in shapes],
        compiler_params=params(),
        cost_estimate=pl.CostEstimate(
            flops=0, bytes_accessed=sum(8 * math.prod(shape) for shape in shapes), transcendentals=0
        ),
        name="lay_out",
    )(scalars, pattern, *[pltpu.with_memory_space_constraint(operand, pltpu.HBM) for operand in operands], after)


def block_sums(parts, first_row, row_count, acc, base, negate):
    size, rhs = parts[0][1][0].shape[1:]
    rows = slice(first_row, first_row + row_count)

    def kernel(*refs):
        refs = list(refs)
        out_ref = refs.pop()
        total = jnp.zeros((row_count * size, rhs), jnp.float32)
        for blocks, values in parts:
            blocks_ref = refs.pop(0)
            place = 0
            for value in values:
                value_ref = refs.pop(0)
                for start in range(0, value.shape[0], 2):
                    right = value_ref[start : start + 2].reshape(2 * size, rhs)
                    left = jnp.concatenate([blocks_ref[place, rows, n] for n in range(2)], axis=2)
                    left = left.reshape(row_count * size, 2 * size)
                    total = total + jnp.dot(left, right, preferred_element_type=jnp.float32)
                    place += 1
        total = total.reshape(row_count, size, rhs)
        if acc is not None:
            total = total + refs.pop(0)[acc[1] : acc[1] + row_count]
        if base is not None:
            total = total - refs.pop(0)[base[1] : base[1] + row_count].astype(jnp.float32)
        out_ref[...] = (-total if negate else total).astype(out_ref.dtype)

    operands = []
    for blocks, values in parts:
        operands += [blocks, *values]
    operands += [extra[0] for extra in (acc, base) if extra is not None]
    blocks_used = 2 * row_count * sum(blocks.shape[0] for blocks, _ in parts)
    return pl.pallas_call(
        kernel,
        out_shape=jax.ShapeDtypeStruct((row_count, size, rhs), jnp.bfloat16 if negate else jnp.float32),
        compiler_params=params(),
        cost_estimate=pl.CostEstimate(
            flops=2 * blocks_used * size * size * rhs, bytes_accessed=2 * blocks_used * size * size, transcendentals=0
        ),
        name="block_sums",
    )(*operands)


def sum_and_solve(gathered, base, inverses, row_start):
    parts, rows, size, rhs = gathered.shape

    def kernel(gathered_ref, *refs):
        refs = list(refs)
        base_ref = refs.pop(0) if base is not None else None
        out_ref = refs.pop()
        for i in range(rows):
            value = gathered_ref[0, i].astype(jnp.float32)
            for part in range(1, parts):
                value = value + gathered_ref[part, i].astype(jnp.float32)
            if base is not None:
                value = value + base_ref[i].astype(jnp.float32)
            value = value.astype(jnp.bfloat16)
            for inverse_ref in refs:
                value = jnp.dot(inverse_ref[i, 0], value, preferred_element_type=jnp.float32).astype(jnp.bfloat16)
            out_ref[i] = value

    operands = [gathered]
    in_specs = [pl.BlockSpec(gathered.shape, lambda g: (0, 0, 0, 0))]
    if base is not None:
        operands.append(base)
        in_specs.append(pl.BlockSpec(base.shape, lambda g: (0, 0, 0)))
    for inverse in inverses:
        operands.append(inverse)
        in_specs.append(pl.BlockSpec((rows, 1, size, size), lambda g: (row_start // rows, 0, 0, 0)))
    return pl.pallas_call(
        kernel,
        grid=(1,),
        in_specs=in_specs,
        out_specs=pl.BlockSpec((rows, size, rhs), lambda g: (0, 0, 0)),
        out_shape=jax.ShapeDtypeStruct((rows, size, rhs), jnp.bfloat16),
        compiler_params=params(),
        cost_estimate=pl.CostEstimate(
            flops=2 * rows * size * size * rhs, bytes_accessed=2 * (parts + 2) * rows * size * rhs, transcendentals=0
        ),
        name="sum_and_solve",
    )(*operands)


def solve_blocks(inverse, values):
    count, size, rhs = values.shape

    def kernel(inverse_ref, value_ref, out_ref):
        for i in range(count):
            out_ref[i] = jnp.dot(inverse_ref[i], value_ref[i], preferred_element_type=jnp.float32).astype(jnp.bfloat16)

    return pl.pallas_call(
        kernel,
        out_shape=jax.ShapeDtypeStruct(values.shape, jnp.bfloat16),
        compiler_params=params(),
        name="solve_blocks",
    )(inverse, values)


def last_solve(scalars, start_index, own, other, inverse, solved, copies):
    count, size, rhs = own.shape

    def kernel(scal, own_ref, other_ref, inverse_ref, solved_ref, out_ref):
        for h in range(count):
            value = (own_ref[h] + other_ref[h].astype(jnp.float32)).astype(jnp.bfloat16)
            value = jnp.dot(inverse_ref[h, 0], value, preferred_element_type=jnp.float32).astype(jnp.bfloat16)
            value = jnp.where(scal[start_index] > 0, value, solved_ref[h])
            for copy in range(copies):
                out_ref[h * copies + copy] = value

    full = lambda g, scal: (0, 0, 0)
    return pl.pallas_call(
        kernel,
        grid_spec=pltpu.PrefetchScalarGridSpec(
            num_scalar_prefetch=1,
            grid=(1,),
            in_specs=[
                pl.BlockSpec(own.shape, full),
                pl.BlockSpec(other.shape, full),
                pl.BlockSpec((count, 1, size, size), lambda g, scal: (0, 0, 0, 0)),
                pl.BlockSpec((count, size, rhs), full),
            ],
            out_specs=pl.BlockSpec((count * copies, size, rhs), full),
        ),
        out_shape=jax.ShapeDtypeStruct((count * copies, size, rhs), jnp.bfloat16),
        compiler_params=params(),
        name="last_solve",
    )(scalars, own, other, inverse, solved)


def on_device(right_sides, factor, pattern, lower_inverse, upper_inverse):
    lo_n = lax.axis_size("lo")
    prow_n = lax.axis_size("hi") * lo_n
    q_n = lax.axis_size("q")
    pcol_n = q_n * lax.axis_size("s")
    row_id = lax.axis_index("hi") * lo_n + lax.axis_index("lo")
    q_id = lax.axis_index("q")
    s_id = lax.axis_index("s")
    col_id = q_id * prow_n + s_id
    row_blocks, _, col_blocks, _, size, _ = factor.shape
    rhs = right_sides.shape[1]
    per = right_sides.shape[0] // size
    spread_n = pcol_n // per
    half = row_blocks // 2
    bounds = (0, half, 3 * row_blocks // 4, 7 * row_blocks // 8, row_blocks)
    cols = tuple(q_n * b for b in bounds)
    device = lambda r, c: r * pcol_n + c
    everyone = [(r, c) for r in range(prow_n) for c in range(pcol_n)]

    is_low = row_id < prow_n // 2
    lo_id = lax.axis_index("lo")
    entries = [q_id, col_id, lo_id, is_low.astype(jnp.int32)]
    scalars = jnp.stack([jnp.asarray(v, jnp.int32) for v in entries])
    pattern = pattern.reshape(row_blocks, col_blocks)
    first_low = half // per

    def route(t, r, c):
        q, s = divmod(c, prow_n)
        up, low = divmod(r, lo_n)
        if t == 0:
            return s, q * prow_n + (1 - up) * lo_n + low
        up = (up + 1 + s // lo_n + q) % 2
        return s, (q + t) % q_n * prow_n + up * lo_n + lo_n - 1 - low

    def spread(values):
        return [
            lax.ppermute(values, ALL_AXES, [(device(r, c), device(*route(t, r, c))) for r, c in everyone])
            for t in range(q_n)
        ]

    def spread_groups(first, last):
        def groups(scal):
            ids = [lax.rem(scal[0] + (q_n - t), q_n) if scal is not None else 0 for t in range(q_n)]
            return [q_n * m + q for q in ids for m in range(first, last, 2)]

        return groups

    def gather(partial):
        return lax.all_gather(partial, ROW_AXES, axis=0)

    def count(level):
        return bounds[level + 1] - bounds[level]

    def part(level, groups, step):
        return (count(level), lambda scal: [bounds[level]], groups, step)

    def laid_out(after, *parts):
        return lay_out(scalars, pattern, factor, after, parts)

    low_starts = lambda scal: [per * lax.rem(scal[2] + t, lo_n) if scal is not None else 0 for t in range(lo_n)]
    low_rows = (half, low_starts)
    late_rows = (count(2) + count(3), lambda scal: [bounds[2]])

    if per == prow_n and pcol_n & (pcol_n - 1) == 0:
        there = [(device(r, c), device(c % prow_n, r * q_n + c // prow_n)) for r, c in everyone]
        back = [(target, source) for source, target in there]
        inverse_rows = lax.dynamic_index_in_dim(
            lower_inverse[:half].reshape(first_low, per, size, size), row_id, 1, keepdims=False
        )
        inverse_rows = lax.ppermute(inverse_rows, ALL_AXES, there)
        blocks = lax.all_to_all(right_sides.reshape(per, size, rhs), ROW_AXES, 0, 0, tiled=True)
        own_zero = solve_blocks(inverse_rows, blocks[:first_low])

        def zero_groups(scal):
            ids = [scal[1] ^ t if scal is not None else 0 for t in range(pcol_n)]
            return [c + pcol_n * r for c in ids for r in range(0, first_low, 2)]

        def exchange(values, t):
            return lax.ppermute(values, ALL_AXES, [(device(r, c), device(r, c ^ t)) for r, c in everyone])

        zero = []
        for t in range(0, pcol_n, 2):
            even = exchange(own_zero, t) if t else own_zero
            zero += [even, exchange(even, 1)]
        (one_zero,) = laid_out(own_zero, part(1, zero_groups, pcol_n))
        zero_step = pcol_n

        rest = lax.ppermute(blocks, ALL_AXES, back)
        owned = (jnp.arange(per) == row_id)[None, :, None, None]
        base = jnp.where(owned, rest[:, None], jnp.zeros((), jnp.bfloat16)).reshape(row_blocks, size, rhs)
    else:
        group_rows = lax.all_gather(right_sides.reshape(per, size, rhs), COL_AXES, axis=0, tiled=True)
        picked = lax.dynamic_index_in_dim(group_rows.reshape(per, pcol_n, size, rhs), col_id, 1, keepdims=False)
        mine = lax.all_gather(picked, ROW_AXES, axis=0, tiled=True)
        own_zero = sum_and_solve(mine[None, :half], None, [lower_inverse], 0)
        zero_groups = spread_groups(0, half)
        zero_step = q_n
        (one_zero,) = laid_out(own_zero, part(1, zero_groups, zero_step))
        zero = spread(own_zero)
        base = jnp.where(row_id == 0, mine, jnp.zeros((), jnp.bfloat16))

    level_groups = [zero_groups] + [spread_groups(bounds[level], bounds[level + 1]) for level in range(1, 4)]
    partial = block_sums([(one_zero, zero)], 0, count(1), None, (base, bounds[1]), True)
    one_rows = sum_and_solve(gather(partial), None, [lower_inverse], bounds[1])
    one = spread(one_rows)
    late_zero, two_one = laid_out(one_rows, (*late_rows, zero_groups, zero_step), part(2, level_groups[1], q_n))
    late = block_sums([(late_zero, zero)], 0, count(2) + count(3), None, (base, bounds[2]), False)
    partial = block_sums([(two_one, one)], 0, count(2), (late, 0), None, True)
    two_rows = sum_and_solve(gather(partial), None, [lower_inverse], bounds[2])
    two = spread(two_rows)
    three_one, three_two, two_three = laid_out(
        two_rows,
        part(3, level_groups[1], q_n),
        part(3, level_groups[2], q_n),
        part(2, level_groups[3], q_n),
    )
    late = block_sums([(three_one, one)], 0, count(3), (late, count(2)), None, False)
    partial = block_sums([(three_two, two)], 0, count(3), (late, 0), None, True)
    three_solved = sum_and_solve(gather(partial), None, [lower_inverse, upper_inverse], bounds[3])
    three = spread(three_solved)
    one_three, one_two, zero_three = laid_out(
        three_solved, part(1, level_groups[3], q_n), part(1, level_groups[2], q_n), (*low_rows, level_groups[3], q_n)
    )
    base_zero = sum_and_solve(base[None, :half], None, [lower_inverse], 0)
    base_zero = lax.dynamic_slice_in_dim(jnp.concatenate([base_zero, base_zero]), per * lo_id, half, 0)
    partial = block_sums([(two_three, three)], 0, count(2), None, None, True)
    two_solved = sum_and_solve(gather(partial), two_rows, [upper_inverse], bounds[2])
    two = spread(two_solved)
    zero_two, zero_one = laid_out(two_solved, (*low_rows, level_groups[2], q_n), (*low_rows, level_groups[1], q_n))
    late = block_sums([(one_three, three)], 0, count(1), None, None, False)
    partial = block_sums([(one_two, two)], 0, count(1), (late, 0), None, True)
    one_solved = sum_and_solve(gather(partial), one_rows, [upper_inverse], bounds[1])
    one = spread(one_solved)
    upper = block_sums([(zero_three, three), (zero_two, two)], 0, half, None, (base_zero, 0), False)
    chunks = [block_sums([(zero_one, one)], t * per, per, (upper, t * per), None, True) for t in range(1, lo_n)]
    own = block_sums([(zero_one, one)], 0, per, (upper, 0), None, True).astype(jnp.float32)
    for t in range(1, lo_n):
        pairs = [((lo, (lo + t) % lo_n)) for lo in range(lo_n)]
        own = own + lax.ppermute(chunks[t - 1], "lo", pairs).astype(jnp.float32)
    other = lax.ppermute(own.astype(jnp.bfloat16), "hi", [(0, 1), (1, 0)])
    solved = jnp.concatenate([one_solved, two_solved, three_solved], axis=0)
    solved = lax.dynamic_slice_in_dim(solved, per * lo_id, per, 0)
    last_inverse = lax.dynamic_slice_in_dim(upper_inverse, per * lo_id, per, 0)
    slots = last_solve(scalars, 3, own, other, last_inverse, solved, spread_n)
    received = lax.all_to_all(slots, COL_AXES, 0, 0, tiled=True)
    mine = lax.dynamic_slice_in_dim(received, lax.rem(col_id, spread_n) * per, per, 0)
    return mine.reshape(per * size, rhs)


def solution(mesh):
    prow_n, pcol_n = mesh.shape["prow"], mesh.shape["pcol"]
    fine = Mesh(mesh.devices.reshape(2, prow_n // 2, pcol_n // prow_n, prow_n), ALL_AXES)
    placed = (
        P(ALL_AXES, None),
        P(None, COL_AXES, None, ROW_AXES, None, None),
        P(None, COL_AXES, None, ROW_AXES),
        P(None, COL_AXES, None, None),
        P(None, COL_AXES, None, None),
    )
    return jax.shard_map(on_device, mesh=fine, in_specs=placed, out_specs=P(ALL_AXES, None), check_vma=False)
```

```python
import math

import jax
import jax.numpy as jnp
from jax import lax
from jax.experimental import pallas as pl
from jax.experimental.pallas import tpu as pltpu
from jax.sharding import Mesh
from jax.sharding import PartitionSpec as P

ROW_AXES = ("hi", "lo")
COL_AXES = ("q", "s")
ALL_AXES = ROW_AXES + COL_AXES
VMEM_LIMIT = 16 * 1024 * 1024


def params():
    return pltpu.CompilerParams(vmem_limit_bytes=VMEM_LIMIT)


def lay_out(scalars, pattern, factor, after, parts):
    size = factor.shape[-1]
    shapes = [(len(groups(None)), rows, 2, size, size) for rows, _, groups, _ in parts]
    copy_count = sum(len(starts(None)) * len(groups(None)) for _, starts, groups, _ in parts)
    steps = sorted({step for _, _, _, step in parts})
    operands = [factor.reshape(factor.shape[0], -1, step, size, size) for step in steps]

    def kernel(scal, pat, *refs):
        factor_refs = dict(zip(steps, refs))
        out_refs = refs[len(steps) + len(after) : -1]
        sems = refs[-1]
        copies = []
        for (rows, starts, groups, step), out_ref in zip(parts, out_refs):
            run = rows // len(starts(scal))
            part_copies = []
            for g, column in enumerate(groups(scal)):
                for n, start in enumerate(starts(scal)):
                    place = sum(map(len, copies)) + len(part_copies)
                    part_copies.append(
                        pltpu.make_async_copy(
                            factor_refs[step].at[
                                pl.ds(start, run), pl.ds(column // step, 2), column % step
                            ],
                            out_ref.at[g, pl.ds(n * run, run)],
                            sems.at[place],
                        )
                    )
            for copy in part_copies:
                copy.start()
            copies.append(part_copies)
        for (rows, starts, groups, step), out_ref, part_copies in zip(parts, out_refs, copies):
            first_rows = starts(scal)
            run = rows // len(first_rows)
            for g, column in enumerate(groups(scal)):
                for n, start in enumerate(first_rows):
                    part_copies[g * len(first_rows) + n].wait()
                    for i in range(run):
                        for k in range(2):

                            @pl.when(pat[start + i, column + k * step] == 0)
                            def _(g=g, n=n, i=i, k=k, run=run, out_ref=out_ref):
                                out_ref[g, n * run + i, k] = jnp.zeros((size, size), jnp.bfloat16)

    return pl.pallas_call(
        kernel,
        grid_spec=pltpu.PrefetchScalarGridSpec(
            num_scalar_prefetch=2,
            grid=(1,),
            in_specs=[pl.BlockSpec(memory_space=pl.ANY)] * (len(steps) + len(after)),
            out_specs=[pl.BlockSpec(memory_space=pltpu.VMEM)] * len(parts),
            scratch_shapes=[pltpu.SemaphoreType.DMA((copy_count,))],
        ),
        out_shape=[jax.ShapeDtypeStruct(shape, jnp.bfloat16) for shape in shapes],
        compiler_params=params(),
        cost_estimate=pl.CostEstimate(
            flops=0, bytes_accessed=sum(8 * math.prod(shape) for shape in shapes), transcendentals=0
        ),
        name="lay_out",
    )(scalars, pattern, *[pltpu.with_memory_space_constraint(operand, pltpu.HBM) for operand in operands], *after)


def block_sums(parts, first_row, row_count, acc, base, negate):
    size, rhs = parts[0][1][0].shape[1:]
    rows = slice(first_row, first_row + row_count)

    def kernel(*refs):
        refs = list(refs)
        out_ref = refs.pop()
        total = jnp.zeros((row_count * size, rhs), jnp.float32)
        for blocks, values in parts:
            blocks_ref = refs.pop(0)
            place = 0
            for value in values:
                value_ref = refs.pop(0)
                for start in range(0, value.shape[0], 2):
                    right = value_ref[start : start + 2].reshape(2 * size, rhs)
                    left = jnp.concatenate([blocks_ref[place, rows, n] for n in range(2)], axis=2)
                    left = left.reshape(row_count * size, 2 * size)
                    total = total + jnp.dot(left, right, preferred_element_type=jnp.float32)
                    place += 1
        total = total.reshape(row_count, size, rhs)
        if acc is not None:
            total = total + refs.pop(0)[acc[1] : acc[1] + row_count]
        if base is not None:
            total = total - refs.pop(0)[base[1] : base[1] + row_count].astype(jnp.float32)
        out_ref[...] = (-total if negate else total).astype(out_ref.dtype)

    operands = []
    for blocks, values in parts:
        operands += [blocks, *values]
    operands += [extra[0] for extra in (acc, base) if extra is not None]
    blocks_used = 2 * row_count * sum(blocks.shape[0] for blocks, _ in parts)
    return pl.pallas_call(
        kernel,
        out_shape=jax.ShapeDtypeStruct((row_count, size, rhs), jnp.bfloat16 if negate else jnp.float32),
        compiler_params=params(),
        cost_estimate=pl.CostEstimate(
            flops=2 * blocks_used * size * size * rhs, bytes_accessed=2 * blocks_used * size * size, transcendentals=0
        ),
        name="block_sums",
    )(*operands)


def sum_and_solve(terms, inverses, row_start):
    rows, size, rhs = terms[0].shape
    term_count = len(terms)

    def kernel(*refs):
        term_refs = refs[:term_count]
        inverse_refs = refs[term_count:-1]
        for i in range(rows):
            value = term_refs[0][i].astype(jnp.float32)
            for ref in term_refs[1:]:
                value = value + ref[i].astype(jnp.float32)
            value = value.astype(jnp.bfloat16)
            for inverse_ref in inverse_refs:
                value = jnp.dot(inverse_ref[i, 0], value, preferred_element_type=jnp.float32).astype(jnp.bfloat16)
            refs[-1][i] = value

    whole = pl.BlockSpec((rows, size, rhs), lambda g: (0, 0, 0))
    inverse = pl.BlockSpec((rows, 1, size, size), lambda g: (row_start // rows, 0, 0, 0))
    return pl.pallas_call(
        kernel,
        grid=(1,),
        in_specs=[whole] * term_count + [inverse] * len(inverses),
        out_specs=whole,
        out_shape=jax.ShapeDtypeStruct((rows, size, rhs), jnp.bfloat16),
        compiler_params=params(),
        cost_estimate=pl.CostEstimate(
            flops=2 * rows * size * size * rhs, bytes_accessed=2 * (term_count + 2) * rows * size * rhs, transcendentals=0
        ),
        name="sum_and_solve",
    )(*terms, *inverses)


def solve_blocks(inverse, values, after):
    count, size, rhs = values.shape

    def kernel(inverse_ref, value_ref, *refs):
        out_ref = refs[-1]
        for i in range(count):
            out_ref[i] = jnp.dot(inverse_ref[i], value_ref[i], preferred_element_type=jnp.float32).astype(jnp.bfloat16)

    return pl.pallas_call(
        kernel,
        in_specs=[pl.BlockSpec(memory_space=pltpu.VMEM)] * 2 + [pl.BlockSpec(memory_space=pl.ANY)] * len(after),
        out_shape=jax.ShapeDtypeStruct(values.shape, jnp.bfloat16),
        compiler_params=params(),
        name="solve_blocks",
    )(inverse, values, *after)


def low_base(scalars, zero, keep, per, q_n, lo_n):
    chunks, size, rhs = zero[0].shape
    scalars = jnp.concatenate([scalars, keep[None].astype(jnp.int32)])

    def kernel(scal, *refs):
        out_ref = refs[-1]
        for h in range(per):
            source = scal[1] ^ (h * q_n + scal[0])
            for r in range(chunks):
                value = jnp.zeros((size, rhs), jnp.bfloat16)
                for t, ref in enumerate(refs[:-1]):
                    value = jnp.where((source == t) & (scal[4] > 0), ref[r], value)
                place = lax.rem(r + lo_n - scal[2], lo_n)
                out_ref[place * per + h] = value

    return pl.pallas_call(
        kernel,
        grid_spec=pltpu.PrefetchScalarGridSpec(
            num_scalar_prefetch=1,
            grid=(1,),
            in_specs=[pl.BlockSpec(memory_space=pltpu.VMEM)] * len(zero),
            out_specs=pl.BlockSpec(memory_space=pltpu.VMEM),
        ),
        out_shape=jax.ShapeDtypeStruct((chunks * per, size, rhs), jnp.bfloat16),
        compiler_params=params(),
        name="low_base",
    )(scalars, *zero)


def last_solve(scalars, start_index, own, other, inverse, solved, copies):
    count, size, rhs = own.shape

    def kernel(scal, own_ref, other_ref, inverse_ref, solved_ref, out_ref):
        for h in range(count):
            value = (own_ref[h] + other_ref[h].astype(jnp.float32)).astype(jnp.bfloat16)
            value = jnp.dot(inverse_ref[h, 0], value, preferred_element_type=jnp.float32).astype(jnp.bfloat16)
            value = jnp.where(scal[start_index] > 0, value, solved_ref[h])
            for copy in range(copies):
                out_ref[h * copies + copy] = value

    full = lambda g, scal: (0, 0, 0)
    return pl.pallas_call(
        kernel,
        grid_spec=pltpu.PrefetchScalarGridSpec(
            num_scalar_prefetch=1,
            grid=(1,),
            in_specs=[
                pl.BlockSpec(own.shape, full),
                pl.BlockSpec(other.shape, full),
                pl.BlockSpec((count, 1, size, size), lambda g, scal: (0, 0, 0, 0)),
                pl.BlockSpec((count, size, rhs), full),
            ],
            out_specs=pl.BlockSpec((count * copies, size, rhs), full),
        ),
        out_shape=jax.ShapeDtypeStruct((count * copies, size, rhs), jnp.bfloat16),
        compiler_params=params(),
        name="last_solve",
    )(scalars, own, other, inverse, solved)


def on_device(right_sides, factor, pattern, lower_inverse, upper_inverse):
    lo_n = lax.axis_size("lo")
    prow_n = lax.axis_size("hi") * lo_n
    q_n = lax.axis_size("q")
    pcol_n = q_n * lax.axis_size("s")
    row_id = lax.axis_index("hi") * lo_n + lax.axis_index("lo")
    q_id = lax.axis_index("q")
    s_id = lax.axis_index("s")
    col_id = q_id * prow_n + s_id
    row_blocks, _, col_blocks, _, size, _ = factor.shape
    rhs = right_sides.shape[1]
    per = right_sides.shape[0] // size
    spread_n = pcol_n // per
    half = row_blocks // 2
    bounds = (0, half, 3 * row_blocks // 4, 7 * row_blocks // 8, row_blocks)
    cols = tuple(q_n * b for b in bounds)
    device = lambda r, c: r * pcol_n + c
    everyone = [(r, c) for r in range(prow_n) for c in range(pcol_n)]

    is_low = row_id < prow_n // 2
    lo_id = lax.axis_index("lo")
    entries = [q_id, col_id, lo_id, is_low.astype(jnp.int32)]
    scalars = jnp.stack([jnp.asarray(v, jnp.int32) for v in entries])
    pattern = pattern.reshape(row_blocks, col_blocks)
    first_low = half // per

    def route(t, r, c):
        q, s = divmod(c, prow_n)
        up, low = divmod(r, lo_n)
        if t == 0:
            return s, q * prow_n + (1 - up) * lo_n + low
        up = (up + 1 + s // lo_n + q) % 2
        return s, (q + t) % q_n * prow_n + up * lo_n + lo_n - 1 - low

    def spread(values):
        return [
            lax.ppermute(values, ALL_AXES, [(device(r, c), device(*route(t, r, c))) for r, c in everyone])
            for t in reversed(range(q_n))
        ][::-1]

    def spread_groups(first, last):
        def groups(scal):
            ids = [lax.rem(scal[0] + (q_n - t), q_n) if scal is not None else 0 for t in range(q_n)]
            return [q_n * m + q for q in ids for m in range(first, last, 2)]

        return groups

    def summands(partial):
        step = 1
        while True:
            pairs = [(device(r, c), device(r ^ step, c)) for r, c in everyone]
            other = lax.ppermute(partial, ALL_AXES, pairs)
            step *= 2
            if step == prow_n:
                return [partial, other]
            partial = partial + other

    def count(level):
        return bounds[level + 1] - bounds[level]

    def part(level, groups, step):
        return (count(level), lambda scal: [bounds[level]], groups, step)

    def laid_out(after, *parts):
        return lay_out(scalars, pattern, factor, after, parts)

    low_starts = lambda scal: [per * lax.rem(scal[2] + t, lo_n) if scal is not None else 0 for t in range(lo_n)]
    low_rows = (half, low_starts)
    late_rows = (count(2) + count(3), lambda scal: [bounds[2]])

    if per == prow_n and pcol_n & (pcol_n - 1) == 0:

        def chunk(r, c):
            q, s = c // prow_n, c % prow_n
            return (r // lo_n + s // lo_n + 1 + q) % 2 * lo_n + r % lo_n

        there = [(device(r, c), device(c % prow_n, chunk(r, c) * q_n + c // prow_n)) for r, c in everyone]
        back = [(target, source) for source, target in there]
        chunk_id = chunk(row_id, col_id)
        inverse_rows = lax.dynamic_index_in_dim(
            lower_inverse[:half].reshape(first_low, per, size, size), chunk_id, 1, keepdims=False
        )

        def zero_groups(scal):
            ids = [scal[1] ^ t if scal is not None else 0 for t in range(pcol_n)]
            return [c + pcol_n * r for c in ids for r in range(0, first_low, 2)]

        def exchange(values, t):
            return lax.ppermute(values, ALL_AXES, [(device(r, c), device(r, c ^ t)) for r, c in everyone])

        inverse_rows, blocks = lax.optimization_barrier((inverse_rows, right_sides.reshape(per, size, rhs)))
        (one_zero,) = laid_out([inverse_rows], part(1, zero_groups, pcol_n))
        inverse_rows = lax.ppermute(inverse_rows, ALL_AXES, there)
        blocks = lax.all_to_all(blocks, ROW_AXES, 0, 0, tiled=True)
        rest = lax.ppermute(blocks[first_low:], ALL_AXES, back)
        own_zero = solve_blocks(inverse_rows, blocks[:first_low], [one_zero])
        even = {t: exchange(own_zero, t) for t in range(pcol_n - 2, 0, -2)}
        even[0] = own_zero
        zero = []
        for t in range(0, pcol_n, 2):
            zero += [even[t], exchange(even[t], 1)]
        zero_step = pcol_n

        owned = (jnp.arange(per) == chunk_id)[None, :, None, None]
        base = jnp.where(owned, rest[:, None], jnp.zeros((), jnp.bfloat16)).reshape(row_blocks - half, size, rhs)
        base_zero = low_base(scalars, zero, row_id == s_id, per, q_n, lo_n)
    else:
        group_rows = lax.all_gather(right_sides.reshape(per, size, rhs), COL_AXES, axis=0, tiled=True)
        picked = lax.dynamic_index_in_dim(group_rows.reshape(per, pcol_n, size, rhs), col_id, 1, keepdims=False)
        mine = lax.all_gather(picked, ROW_AXES, axis=0, tiled=True)
        own_zero = sum_and_solve([mine[:half]], [lower_inverse], 0)
        zero_groups = spread_groups(0, half)
        zero_step = q_n
        (one_zero,) = laid_out([own_zero], part(1, zero_groups, zero_step))
        zero = spread(own_zero)
        base = jnp.where(row_id == 0, mine[half:], jnp.zeros((), jnp.bfloat16))
        base_zero = jnp.where(row_id == 0, own_zero, jnp.zeros((), jnp.bfloat16))
        base_zero = lax.dynamic_slice_in_dim(jnp.concatenate([base_zero, base_zero]), per * lo_id, half, 0)

    level_groups = [zero_groups] + [spread_groups(bounds[level], bounds[level + 1]) for level in range(1, 4)]
    partial = block_sums([(one_zero, zero)], 0, count(1), None, (base, 0), True)
    one_rows = sum_and_solve(summands(partial), [lower_inverse], bounds[1])
    one = spread(one_rows)
    late_zero, two_one = laid_out([one_rows, base_zero], (*late_rows, zero_groups, zero_step), part(2, level_groups[1], q_n))
    late = block_sums([(late_zero, zero)], 0, count(2) + count(3), None, (base, bounds[2] - half), False)
    partial = block_sums([(two_one, one)], 0, count(2), (late, 0), None, True)
    two_rows = sum_and_solve(summands(partial), [lower_inverse], bounds[2])
    two = spread(two_rows)
    three_one, three_two = laid_out([two_rows], part(3, level_groups[1], q_n), part(3, level_groups[2], q_n))
    late = block_sums([(three_one, one)], 0, count(3), (late, count(2)), None, False)
    partial = block_sums([(three_two, two)], 0, count(3), (late, 0), None, True)
    three_solved = sum_and_solve(summands(partial), [lower_inverse, upper_inverse], bounds[3])
    three = spread(three_solved)
    two_three, one_three, one_two, zero_three = laid_out(
        [three_solved],
        part(2, level_groups[3], q_n),
        part(1, level_groups[3], q_n),
        part(1, level_groups[2], q_n),
        (*low_rows, level_groups[3], q_n),
    )
    partial = block_sums([(two_three, three)], 0, count(2), None, None, True)
    two_solved = sum_and_solve(summands(partial) + [two_rows], [upper_inverse], bounds[2])
    two = spread(two_solved)
    zero_two, zero_one = laid_out([two_solved], (*low_rows, level_groups[2], q_n), (*low_rows, level_groups[1], q_n))
    late = block_sums([(one_three, three)], 0, count(1), None, None, False)
    partial = block_sums([(one_two, two)], 0, count(1), (late, 0), None, True)
    one_solved = sum_and_solve(summands(partial) + [one_rows], [upper_inverse], bounds[1])
    one = spread(one_solved)
    upper = block_sums([(zero_three, three), (zero_two, two)], 0, half, None, (base_zero, 0), False)
    chunks = [block_sums([(zero_one, one)], t * per, per, (upper, t * per), None, True) for t in range(1, lo_n)]
    own = block_sums([(zero_one, one)], 0, per, (upper, 0), None, True).astype(jnp.float32)
    for t in range(1, lo_n):
        pairs = [((lo, (lo + t) % lo_n)) for lo in range(lo_n)]
        own = own + lax.ppermute(chunks[t - 1], "lo", pairs).astype(jnp.float32)
    other = lax.ppermute(own.astype(jnp.bfloat16), "hi", [(0, 1), (1, 0)])
    solved = jnp.concatenate([one_solved, two_solved, three_solved], axis=0)
    solved = lax.dynamic_slice_in_dim(solved, per * lo_id, per, 0)
    last_inverse = lax.dynamic_slice_in_dim(upper_inverse, per * lo_id, per, 0)
    slots = last_solve(scalars, 3, own, other, last_inverse, solved, spread_n)
    received = lax.all_to_all(slots, COL_AXES, 0, 0, tiled=True)
    mine = lax.dynamic_slice_in_dim(received, lax.rem(col_id, spread_n) * per, per, 0)
    return mine.reshape(per * size, rhs)


def solution(mesh):
    prow_n, pcol_n = mesh.shape["prow"], mesh.shape["pcol"]
    fine = Mesh(mesh.devices.reshape(2, prow_n // 2, pcol_n // prow_n, prow_n), ALL_AXES)
    placed = (
        P(ALL_AXES, None),
        P(None, COL_AXES, None, ROW_AXES, None, None),
        P(None, COL_AXES, None, ROW_AXES),
        P(None, COL_AXES, None, None),
        P(None, COL_AXES, None, None),
    )
    return jax.shard_map(on_device, mesh=fine, in_specs=placed, out_specs=P(ALL_AXES, None), check_vma=False)
```

```python
import math

import jax
import jax.numpy as jnp
from jax import lax
from jax.experimental import pallas as pl
from jax.experimental.pallas import tpu as pltpu
from jax.sharding import Mesh
from jax.sharding import PartitionSpec as P

ROW_AXES = ("hi", "lo")
COL_AXES = ("q", "s")
ALL_AXES = ROW_AXES + COL_AXES
VMEM_LIMIT = 16 * 1024 * 1024


def params():
    return pltpu.CompilerParams(vmem_limit_bytes=VMEM_LIMIT)


def lay_out(scalars, pattern, factor, after, parts):
    size = factor.shape[-1]
    shapes = [(len(groups(None)), rows, 2, size, size) for rows, _, groups, _ in parts]
    copy_count = sum(len(starts(None)) * len(groups(None)) for _, starts, groups, _ in parts)
    steps = sorted({step for _, _, _, step in parts})
    operands = [factor.reshape(factor.shape[0], -1, step, size, size) for step in steps]

    def kernel(scal, pat, *refs):
        factor_refs = dict(zip(steps, refs))
        out_refs = refs[len(steps) + len(after) : -1]
        sems = refs[-1]
        copies = []
        for (rows, starts, groups, step), out_ref in zip(parts, out_refs):
            run = rows // len(starts(scal))
            part_copies = []
            for g, column in enumerate(groups(scal)):
                for n, start in enumerate(starts(scal)):
                    place = sum(map(len, copies)) + len(part_copies)
                    part_copies.append(
                        pltpu.make_async_copy(
                            factor_refs[step].at[
                                pl.ds(start, run), pl.ds(column // step, 2), column % step
                            ],
                            out_ref.at[g, pl.ds(n * run, run)],
                            sems.at[place],
                        )
                    )
            for copy in part_copies:
                copy.start()
            copies.append(part_copies)
        for (rows, starts, groups, step), out_ref, part_copies in zip(parts, out_refs, copies):
            first_rows = starts(scal)
            run = rows // len(first_rows)
            for g, column in enumerate(groups(scal)):
                for n, start in enumerate(first_rows):
                    part_copies[g * len(first_rows) + n].wait()
                    for i in range(run):
                        for k in range(2):

                            @pl.when(pat[start + i, column + k * step] == 0)
                            def _(g=g, n=n, i=i, k=k, run=run, out_ref=out_ref):
                                out_ref[g, n * run + i, k] = jnp.zeros((size, size), jnp.bfloat16)

    return pl.pallas_call(
        kernel,
        grid_spec=pltpu.PrefetchScalarGridSpec(
            num_scalar_prefetch=2,
            grid=(1,),
            in_specs=[pl.BlockSpec(memory_space=pl.ANY)] * (len(steps) + len(after)),
            out_specs=[pl.BlockSpec(memory_space=pltpu.VMEM)] * len(parts),
            scratch_shapes=[pltpu.SemaphoreType.DMA((copy_count,))],
        ),
        out_shape=[jax.ShapeDtypeStruct(shape, jnp.bfloat16) for shape in shapes],
        compiler_params=params(),
        cost_estimate=pl.CostEstimate(
            flops=0, bytes_accessed=sum(8 * math.prod(shape) for shape in shapes), transcendentals=0
        ),
        name="lay_out",
    )(scalars, pattern, *[pltpu.with_memory_space_constraint(operand, pltpu.HBM) for operand in operands], *after)


def block_sums(parts, first_row, row_count, acc, base, negate):
    size, rhs = parts[0][1][0].shape[1:]
    rows = slice(first_row, first_row + row_count)

    def kernel(*refs):
        refs = list(refs)
        out_ref = refs.pop()
        total = jnp.zeros((row_count * size, rhs), jnp.float32)
        for blocks, values in parts:
            blocks_ref = refs.pop(0)
            place = 0
            for value in values:
                value_ref = refs.pop(0)
                for start in range(0, value.shape[0], 2):
                    right = value_ref[start : start + 2].reshape(2 * size, rhs)
                    left = jnp.concatenate([blocks_ref[place, rows, n] for n in range(2)], axis=2)
                    left = left.reshape(row_count * size, 2 * size)
                    total = total + jnp.dot(left, right, preferred_element_type=jnp.float32)
                    place += 1
        total = total.reshape(row_count, size, rhs)
        if acc is not None:
            total = total + refs.pop(0)[acc[1] : acc[1] + row_count]
        if base is not None:
            total = total - refs.pop(0)[base[1] : base[1] + row_count].astype(jnp.float32)
        out_ref[...] = (-total if negate else total).astype(out_ref.dtype)

    operands = []
    for blocks, values in parts:
        operands += [blocks, *values]
    operands += [extra[0] for extra in (acc, base) if extra is not None]
    blocks_used = 2 * row_count * sum(blocks.shape[0] for blocks, _ in parts)
    return pl.pallas_call(
        kernel,
        out_shape=jax.ShapeDtypeStruct((row_count, size, rhs), jnp.bfloat16 if negate else jnp.float32),
        compiler_params=params(),
        cost_estimate=pl.CostEstimate(
            flops=2 * blocks_used * size * size * rhs, bytes_accessed=2 * blocks_used * size * size, transcendentals=0
        ),
        name="block_sums",
    )(*operands)


def low_sums(blocks, values, acc, chunks):
    rows, size, rhs = acc.shape

    def kernel(blocks_ref, *refs):
        value_refs, acc_ref, out_refs = refs[: len(values)], refs[len(values)], refs[len(values) + 1 :]
        total = acc_ref[...].reshape(rows * size, rhs)
        place = 0
        for value, ref in zip(values, value_refs):
            for start in range(0, value.shape[0], 2):
                left = jnp.concatenate([blocks_ref[place, :, n] for n in range(2)], axis=2)
                right = ref[start : start + 2].reshape(2 * size, rhs)
                total = total + jnp.dot(
                    left.reshape(rows * size, 2 * size), right, preferred_element_type=jnp.float32
                )
                place += 1
        total = (-total).astype(jnp.bfloat16).reshape(chunks, rows // chunks, size, rhs)
        for n, ref in enumerate(out_refs):
            ref[...] = total[n]

    return pl.pallas_call(
        kernel,
        out_shape=[jax.ShapeDtypeStruct((rows // chunks, size, rhs), jnp.bfloat16)] * chunks,
        compiler_params=params(),
        name="low_sums",
    )(blocks, *values, acc)


def sum_and_solve(terms, inverses, row_start):
    rows, size, rhs = terms[0].shape
    term_count = len(terms)

    def kernel(*refs):
        term_refs = refs[:term_count]
        inverse_refs = refs[term_count:-1]
        for i in range(rows):
            value = term_refs[0][i].astype(jnp.float32)
            for ref in term_refs[1:]:
                value = value + ref[i].astype(jnp.float32)
            value = value.astype(jnp.bfloat16)
            for inverse_ref in inverse_refs:
                value = jnp.dot(inverse_ref[i, 0], value, preferred_element_type=jnp.float32).astype(jnp.bfloat16)
            refs[-1][i] = value

    whole = pl.BlockSpec((rows, size, rhs), lambda g: (0, 0, 0))
    inverse = pl.BlockSpec((rows, 1, size, size), lambda g: (row_start // rows, 0, 0, 0))
    return pl.pallas_call(
        kernel,
        grid=(1,),
        in_specs=[whole] * term_count + [inverse] * len(inverses),
        out_specs=whole,
        out_shape=jax.ShapeDtypeStruct((rows, size, rhs), jnp.bfloat16),
        compiler_params=params(),
        cost_estimate=pl.CostEstimate(
            flops=2 * rows * size * size * rhs, bytes_accessed=2 * (term_count + 2) * rows * size * rhs, transcendentals=0
        ),
        name="sum_and_solve",
    )(*terms, *inverses)


def solve_blocks(inverse, values, after):
    count, size, rhs = values.shape

    def kernel(inverse_ref, value_ref, *refs):
        out_ref = refs[-1]
        for i in range(count):
            out_ref[i] = jnp.dot(inverse_ref[i], value_ref[i], preferred_element_type=jnp.float32).astype(jnp.bfloat16)

    return pl.pallas_call(
        kernel,
        in_specs=[pl.BlockSpec(memory_space=pltpu.VMEM)] * 2 + [pl.BlockSpec(memory_space=pl.ANY)] * len(after),
        out_shape=jax.ShapeDtypeStruct(values.shape, jnp.bfloat16),
        compiler_params=params(),
        name="solve_blocks",
    )(inverse, values, *after)


def low_base(scalars, zero, keep, per, q_n, lo_n):
    chunks, size, rhs = zero[0].shape
    scalars = jnp.concatenate([scalars, keep[None].astype(jnp.int32)])

    def kernel(scal, *refs):
        out_ref = refs[-1]
        for h in range(per):
            source = scal[1] ^ (h * q_n + scal[0])
            for r in range(chunks):
                value = jnp.zeros((size, rhs), jnp.bfloat16)
                for t, ref in enumerate(refs[:-1]):
                    value = jnp.where((source == t) & (scal[4] > 0), ref[r], value)
                place = lax.rem(r + lo_n - scal[2], lo_n)
                out_ref[place * per + h] = value

    return pl.pallas_call(
        kernel,
        grid_spec=pltpu.PrefetchScalarGridSpec(
            num_scalar_prefetch=1,
            grid=(1,),
            in_specs=[pl.BlockSpec(memory_space=pltpu.VMEM)] * len(zero),
            out_specs=pl.BlockSpec(memory_space=pltpu.VMEM),
        ),
        out_shape=jax.ShapeDtypeStruct((chunks * per, size, rhs), jnp.bfloat16),
        compiler_params=params(),
        name="low_base",
    )(scalars, *zero)


def last_solve(scalars, start_index, own, other, inverse, solved, copies):
    count, size, rhs = own.shape

    def kernel(scal, own_ref, other_ref, inverse_ref, solved_ref, out_ref):
        for h in range(count):
            value = (own_ref[h] + other_ref[h].astype(jnp.float32)).astype(jnp.bfloat16)
            value = jnp.dot(inverse_ref[h, 0], value, preferred_element_type=jnp.float32).astype(jnp.bfloat16)
            value = jnp.where(scal[start_index] > 0, value, solved_ref[h])
            for copy in range(copies):
                out_ref[h * copies + copy] = value

    full = lambda g, scal: (0, 0, 0)
    return pl.pallas_call(
        kernel,
        grid_spec=pltpu.PrefetchScalarGridSpec(
            num_scalar_prefetch=1,
            grid=(1,),
            in_specs=[
                pl.BlockSpec(own.shape, full),
                pl.BlockSpec(other.shape, full),
                pl.BlockSpec((count, 1, size, size), lambda g, scal: (0, 0, 0, 0)),
                pl.BlockSpec((count, size, rhs), full),
            ],
            out_specs=pl.BlockSpec((count * copies, size, rhs), full),
        ),
        out_shape=jax.ShapeDtypeStruct((count * copies, size, rhs), jnp.bfloat16),
        compiler_params=params(),
        name="last_solve",
    )(scalars, own, other, inverse, solved)


def on_device(right_sides, factor, pattern, lower_inverse, upper_inverse):
    lo_n = lax.axis_size("lo")
    prow_n = lax.axis_size("hi") * lo_n
    q_n = lax.axis_size("q")
    pcol_n = q_n * lax.axis_size("s")
    row_id = lax.axis_index("hi") * lo_n + lax.axis_index("lo")
    q_id = lax.axis_index("q")
    s_id = lax.axis_index("s")
    col_id = q_id * prow_n + s_id
    row_blocks, _, col_blocks, _, size, _ = factor.shape
    rhs = right_sides.shape[1]
    per = right_sides.shape[0] // size
    spread_n = pcol_n // per
    half = row_blocks // 2
    bounds = (0, half, 3 * row_blocks // 4, 7 * row_blocks // 8, row_blocks)
    cols = tuple(q_n * b for b in bounds)
    device = lambda r, c: r * pcol_n + c
    everyone = [(r, c) for r in range(prow_n) for c in range(pcol_n)]

    is_low = row_id < prow_n // 2
    lo_id = lax.axis_index("lo")
    entries = [q_id, col_id, lo_id, is_low.astype(jnp.int32)]
    scalars = jnp.stack([jnp.asarray(v, jnp.int32) for v in entries])
    pattern = pattern.reshape(row_blocks, col_blocks)
    first_low = half // per

    def route(t, r, c):
        q, s = divmod(c, prow_n)
        up, low = divmod(r, lo_n)
        if t == 0:
            return s, q * prow_n + (1 - up) * lo_n + low
        up = (up + 1 + s // lo_n + q) % 2
        return s, (q + t) % q_n * prow_n + up * lo_n + lo_n - 1 - low

    def spread(values):
        return [
            lax.ppermute(values, ALL_AXES, [(device(r, c), device(*route(t, r, c))) for r, c in everyone])
            for t in reversed(range(q_n))
        ][::-1]

    def spread_groups(first, last):
        def groups(scal):
            ids = [lax.rem(scal[0] + (q_n - t), q_n) if scal is not None else 0 for t in range(q_n)]
            return [q_n * m + q for q in ids for m in range(first, last, 2)]

        return groups

    def summands(partial):
        step = prow_n // 2
        while True:
            pairs = [(device(r, c), device(r ^ step, c)) for r, c in everyone]
            other = lax.ppermute(partial, ALL_AXES, pairs)
            step //= 2
            if step == 0:
                return [partial, other]
            partial = partial + other

    def count(level):
        return bounds[level + 1] - bounds[level]

    def part(level, groups, step):
        return (count(level), lambda scal: [bounds[level]], groups, step)

    def laid_out(after, *parts):
        return lay_out(scalars, pattern, factor, after, parts)

    low_starts = lambda scal: [per * lax.rem(scal[2] + t, lo_n) if scal is not None else 0 for t in range(lo_n)]
    low_rows = (half, low_starts)
    late_rows = (count(2) + count(3), lambda scal: [bounds[2]])

    if per == prow_n and pcol_n & (pcol_n - 1) == 0:

        def chunk(r, c):
            q, s = c // prow_n, c % prow_n
            return (r // lo_n + s // lo_n + 1 + q) % 2 * lo_n + r % lo_n

        there = [(device(r, c), device(c % prow_n, chunk(r, c) * q_n + c // prow_n)) for r, c in everyone]
        back = [(target, source) for source, target in there]
        chunk_id = chunk(row_id, col_id)
        inverse_rows = lax.dynamic_index_in_dim(
            lower_inverse[:half].reshape(first_low, per, size, size), chunk_id, 1, keepdims=False
        )

        def zero_groups(scal):
            ids = [scal[1] ^ t if scal is not None else 0 for t in range(pcol_n)]
            return [c + pcol_n * r for c in ids for r in range(0, first_low, 2)]

        def exchange(values, t):
            return lax.ppermute(values, ALL_AXES, [(device(r, c), device(r, c ^ t)) for r, c in everyone])

        inverse_rows, blocks = lax.optimization_barrier((inverse_rows, right_sides.reshape(per, size, rhs)))
        (one_zero,) = laid_out([inverse_rows], part(1, zero_groups, pcol_n))
        inverse_rows = lax.ppermute(inverse_rows, ALL_AXES, there)
        blocks = lax.all_to_all(blocks, ROW_AXES, 0, 0, tiled=True)
        rest = lax.ppermute(blocks[first_low:], ALL_AXES, back)
        own_zero = solve_blocks(inverse_rows, blocks[:first_low], [one_zero])
        even = {t: exchange(own_zero, t) for t in range(pcol_n - 2, 0, -2)}
        even[0] = own_zero
        zero = []
        for t in range(0, pcol_n, 2):
            zero += [even[t], exchange(even[t], 1)]
        zero_step = pcol_n

        owned = (jnp.arange(per) == chunk_id)[None, :, None, None]
        base = jnp.where(owned, rest[:, None], jnp.zeros((), jnp.bfloat16)).reshape(row_blocks - half, size, rhs)
        base_zero = low_base(scalars, zero, row_id == s_id, per, q_n, lo_n)
    else:
        group_rows = lax.all_gather(right_sides.reshape(per, size, rhs), COL_AXES, axis=0, tiled=True)
        picked = lax.dynamic_index_in_dim(group_rows.reshape(per, pcol_n, size, rhs), col_id, 1, keepdims=False)
        mine = lax.all_gather(picked, ROW_AXES, axis=0, tiled=True)
        own_zero = sum_and_solve([mine[:half]], [lower_inverse], 0)
        zero_groups = spread_groups(0, half)
        zero_step = q_n
        (one_zero,) = laid_out([own_zero], part(1, zero_groups, zero_step))
        zero = spread(own_zero)
        base = jnp.where(row_id == 0, mine[half:], jnp.zeros((), jnp.bfloat16))
        base_zero = jnp.where(row_id == 0, own_zero, jnp.zeros((), jnp.bfloat16))
        base_zero = lax.dynamic_slice_in_dim(jnp.concatenate([base_zero, base_zero]), per * lo_id, half, 0)

    level_groups = [zero_groups] + [spread_groups(bounds[level], bounds[level + 1]) for level in range(1, 4)]
    partial = block_sums([(one_zero, zero)], 0, count(1), None, (base, 0), True)
    one_rows = sum_and_solve(summands(partial), [lower_inverse], bounds[1])
    one = spread(one_rows)
    late_zero, two_one = laid_out([one_rows, base_zero], (*late_rows, zero_groups, zero_step), part(2, level_groups[1], q_n))
    late = block_sums([(late_zero, zero)], 0, count(2) + count(3), None, (base, bounds[2] - half), False)
    partial = block_sums([(two_one, one)], 0, count(2), (late, 0), None, True)
    two_rows = sum_and_solve(summands(partial), [lower_inverse], bounds[2])
    two = spread(two_rows)
    three_one, three_two = laid_out([two_rows], part(3, level_groups[1], q_n), part(3, level_groups[2], q_n))
    late = block_sums([(three_one, one)], 0, count(3), (late, count(2)), None, False)
    partial = block_sums([(three_two, two)], 0, count(3), (late, 0), None, True)
    three_solved = sum_and_solve(summands(partial), [lower_inverse, upper_inverse], bounds[3])
    three = spread(three_solved)
    two_three, one_three, one_two, zero_three = laid_out(
        [three_solved],
        part(2, level_groups[3], q_n),
        part(1, level_groups[3], q_n),
        part(1, level_groups[2], q_n),
        (*low_rows, level_groups[3], q_n),
    )
    partial = block_sums([(two_three, three)], 0, count(2), None, None, True)
    two_solved = sum_and_solve(summands(partial) + [two_rows], [upper_inverse], bounds[2])
    two = spread(two_solved)
    zero_two, zero_one = laid_out([two_solved], (*low_rows, level_groups[2], q_n), (*low_rows, level_groups[1], q_n))
    late = block_sums([(one_three, three)], 0, count(1), None, None, False)
    partial = block_sums([(one_two, two)], 0, count(1), (late, 0), None, True)
    one_solved = sum_and_solve(summands(partial) + [one_rows], [upper_inverse], bounds[1])
    one = spread(one_solved)
    upper = block_sums([(zero_three, three), (zero_two, two)], 0, half, None, (base_zero, 0), False)
    own, *chunks = low_sums(zero_one, one, upper, lo_n)
    own = own.astype(jnp.float32)
    for t in range(1, lo_n):
        pairs = [((lo, (lo + t) % lo_n)) for lo in range(lo_n)]
        own = own + lax.ppermute(chunks[t - 1], "lo", pairs).astype(jnp.float32)
    other = lax.ppermute(own.astype(jnp.bfloat16), "hi", [(0, 1), (1, 0)])
    solved = jnp.concatenate([one_solved, two_solved, three_solved], axis=0)
    solved = lax.dynamic_slice_in_dim(solved, per * lo_id, per, 0)
    last_inverse = lax.dynamic_slice_in_dim(upper_inverse, per * lo_id, per, 0)
    slots = last_solve(scalars, 3, own, other, last_inverse, solved, spread_n)
    received = lax.all_to_all(slots, COL_AXES, 0, 0, tiled=True)
    mine = lax.dynamic_slice_in_dim(received, lax.rem(col_id, spread_n) * per, per, 0)
    return mine.reshape(per * size, rhs)


def solution(mesh):
    prow_n, pcol_n = mesh.shape["prow"], mesh.shape["pcol"]
    fine = Mesh(mesh.devices.reshape(2, prow_n // 2, pcol_n // prow_n, prow_n), ALL_AXES)
    placed = (
        P(ALL_AXES, None),
        P(None, COL_AXES, None, ROW_AXES, None, None),
        P(None, COL_AXES, None, ROW_AXES),
        P(None, COL_AXES, None, None),
        P(None, COL_AXES, None, None),
    )
    return jax.shard_map(on_device, mesh=fine, in_specs=placed, out_specs=P(ALL_AXES, None), check_vma=False)
```

```python
import math

import jax
import jax.numpy as jnp
from jax import lax
from jax.experimental import pallas as pl
from jax.experimental.pallas import tpu as pltpu
from jax.sharding import Mesh
from jax.sharding import PartitionSpec as P

ROW_AXES = ("hi", "lo")
COL_AXES = ("q", "s")
ALL_AXES = ROW_AXES + COL_AXES
VMEM_LIMIT = 16 * 1024 * 1024


def params():
    return pltpu.CompilerParams(vmem_limit_bytes=VMEM_LIMIT)


def lay_out(scalars, pattern, factor, after, parts):
    size = factor.shape[-1]
    shapes = [(len(groups(None)), rows, 2, size, size) for rows, _, groups, _ in parts]
    copy_count = sum(len(starts(None)) * len(groups(None)) for _, starts, groups, _ in parts)
    steps = sorted({step for _, _, _, step in parts})
    operands = [factor.reshape(factor.shape[0], -1, step, size, size) for step in steps]

    def kernel(scal, pat, *refs):
        factor_refs = dict(zip(steps, refs))
        out_refs = refs[len(steps) + len(after) : -1]
        sems = refs[-1]
        copies = []
        for (rows, starts, groups, step), out_ref in zip(parts, out_refs):
            run = rows // len(starts(scal))
            part_copies = []
            for g, column in enumerate(groups(scal)):
                for n, start in enumerate(starts(scal)):
                    place = sum(map(len, copies)) + len(part_copies)
                    part_copies.append(
                        pltpu.make_async_copy(
                            factor_refs[step].at[
                                pl.ds(start, run), pl.ds(column // step, 2), column % step
                            ],
                            out_ref.at[g, pl.ds(n * run, run)],
                            sems.at[place],
                        )
                    )
            for copy in part_copies:
                copy.start()
            copies.append(part_copies)
        for (rows, starts, groups, step), out_ref, part_copies in zip(parts, out_refs, copies):
            first_rows = starts(scal)
            run = rows // len(first_rows)
            for g, column in enumerate(groups(scal)):
                for n, start in enumerate(first_rows):
                    part_copies[g * len(first_rows) + n].wait()
                    for i in range(run):
                        for k in range(2):

                            @pl.when(pat[start + i, column + k * step] == 0)
                            def _(g=g, n=n, i=i, k=k, run=run, out_ref=out_ref):
                                out_ref[g, n * run + i, k] = jnp.zeros((size, size), jnp.bfloat16)

    return pl.pallas_call(
        kernel,
        grid_spec=pltpu.PrefetchScalarGridSpec(
            num_scalar_prefetch=2,
            grid=(1,),
            in_specs=[pl.BlockSpec(memory_space=pl.ANY)] * (len(steps) + len(after)),
            out_specs=[pl.BlockSpec(memory_space=pltpu.VMEM)] * len(parts),
            scratch_shapes=[pltpu.SemaphoreType.DMA((copy_count,))],
        ),
        out_shape=[jax.ShapeDtypeStruct(shape, jnp.bfloat16) for shape in shapes],
        compiler_params=params(),
        cost_estimate=pl.CostEstimate(
            flops=0, bytes_accessed=sum(8 * math.prod(shape) for shape in shapes), transcendentals=0
        ),
        name="lay_out",
    )(scalars, pattern, *[pltpu.with_memory_space_constraint(operand, pltpu.HBM) for operand in operands], *after)


def block_sums(parts, first_row, row_count, acc, base, negate):
    size, rhs = parts[0][1][0].shape[1:]
    rows = slice(first_row, first_row + row_count)

    def kernel(*refs):
        refs = list(refs)
        out_ref = refs.pop()
        total = jnp.zeros((row_count * size, rhs), jnp.float32)
        for blocks, values in parts:
            blocks_ref = refs.pop(0)
            place = 0
            for value in values:
                value_ref = refs.pop(0)
                for start in range(0, value.shape[0], 2):
                    right = value_ref[start : start + 2].reshape(2 * size, rhs)
                    left = jnp.concatenate([blocks_ref[place, rows, n] for n in range(2)], axis=2)
                    left = left.reshape(row_count * size, 2 * size)
                    total = total + jnp.dot(left, right, preferred_element_type=jnp.float32)
                    place += 1
        total = total.reshape(row_count, size, rhs)
        if acc is not None:
            total = total + refs.pop(0)[acc[1] : acc[1] + row_count]
        if base is not None:
            total = total - refs.pop(0)[base[1] : base[1] + row_count].astype(jnp.float32)
        out_ref[...] = (-total if negate else total).astype(out_ref.dtype)

    operands = []
    for blocks, values in parts:
        operands += [blocks, *values]
    operands += [extra[0] for extra in (acc, base) if extra is not None]
    blocks_used = 2 * row_count * sum(blocks.shape[0] for blocks, _ in parts)
    return pl.pallas_call(
        kernel,
        out_shape=jax.ShapeDtypeStruct((row_count, size, rhs), jnp.bfloat16 if negate else jnp.float32),
        compiler_params=params(),
        cost_estimate=pl.CostEstimate(
            flops=2 * blocks_used * size * size * rhs, bytes_accessed=2 * blocks_used * size * size, transcendentals=0
        ),
        name="block_sums",
    )(*operands)


def low_sums(blocks, values, acc, chunks):
    rows, size, rhs = acc.shape

    def kernel(blocks_ref, *refs):
        value_refs, acc_ref, out_refs = refs[: len(values)], refs[len(values)], refs[len(values) + 1 :]
        total = acc_ref[...].reshape(rows * size, rhs)
        place = 0
        for value, ref in zip(values, value_refs):
            for start in range(0, value.shape[0], 2):
                left = jnp.concatenate([blocks_ref[place, :, n] for n in range(2)], axis=2)
                right = ref[start : start + 2].reshape(2 * size, rhs)
                total = total + jnp.dot(
                    left.reshape(rows * size, 2 * size), right, preferred_element_type=jnp.float32
                )
                place += 1
        total = (-total).astype(jnp.bfloat16).reshape(chunks, rows // chunks, size, rhs)
        for n, ref in enumerate(out_refs):
            ref[...] = total[n]

    return pl.pallas_call(
        kernel,
        out_shape=[jax.ShapeDtypeStruct((rows // chunks, size, rhs), jnp.bfloat16)] * chunks,
        compiler_params=params(),
        name="low_sums",
    )(blocks, *values, acc)


def sum_and_solve(terms, inverses, row_start):
    rows, size, rhs = terms[0].shape
    term_count = len(terms)

    def kernel(*refs):
        term_refs = refs[:term_count]
        inverse_refs = refs[term_count:-1]
        for i in range(rows):
            value = term_refs[0][i].astype(jnp.float32)
            for ref in term_refs[1:]:
                value = value + ref[i].astype(jnp.float32)
            value = value.astype(jnp.bfloat16)
            for inverse_ref in inverse_refs:
                value = jnp.dot(inverse_ref[i, 0], value, preferred_element_type=jnp.float32).astype(jnp.bfloat16)
            refs[-1][i] = value

    whole = pl.BlockSpec((rows, size, rhs), lambda g: (0, 0, 0))
    inverse = pl.BlockSpec((rows, 1, size, size), lambda g: (row_start // rows, 0, 0, 0))
    return pl.pallas_call(
        kernel,
        grid=(1,),
        in_specs=[whole] * term_count + [inverse] * len(inverses),
        out_specs=whole,
        out_shape=jax.ShapeDtypeStruct((rows, size, rhs), jnp.bfloat16),
        compiler_params=params(),
        cost_estimate=pl.CostEstimate(
            flops=2 * rows * size * size * rhs, bytes_accessed=2 * (term_count + 2) * rows * size * rhs, transcendentals=0
        ),
        name="sum_and_solve",
    )(*terms, *inverses)


def solve_blocks(inverse, values, after):
    count, size, rhs = values.shape

    def kernel(inverse_ref, value_ref, *refs):
        out_ref = refs[-1]
        for i in range(count):
            out_ref[i] = jnp.dot(inverse_ref[i], value_ref[i], preferred_element_type=jnp.float32).astype(jnp.bfloat16)

    return pl.pallas_call(
        kernel,
        in_specs=[pl.BlockSpec(memory_space=pltpu.VMEM)] * 2 + [pl.BlockSpec(memory_space=pl.ANY)] * len(after),
        out_shape=jax.ShapeDtypeStruct(values.shape, jnp.bfloat16),
        compiler_params=params(),
        name="solve_blocks",
    )(inverse, values, *after)


def low_base(scalars, zero, keep, per, q_n, lo_n):
    chunks, size, rhs = zero[0].shape
    scalars = jnp.concatenate([scalars, keep[None].astype(jnp.int32)])

    def kernel(scal, *refs):
        out_ref = refs[-1]
        for h in range(per):
            source = scal[1] ^ (h * q_n + scal[0])
            for r in range(chunks):
                value = jnp.zeros((size, rhs), jnp.bfloat16)
                for t, ref in enumerate(refs[:-1]):
                    value = jnp.where((source == t) & (scal[3] > 0), ref[r], value)
                place = lax.rem(r + lo_n - scal[2], lo_n)
                out_ref[place * per + h] = value

    return pl.pallas_call(
        kernel,
        grid_spec=pltpu.PrefetchScalarGridSpec(
            num_scalar_prefetch=1,
            grid=(1,),
            in_specs=[pl.BlockSpec(memory_space=pltpu.VMEM)] * len(zero),
            out_specs=pl.BlockSpec(memory_space=pltpu.VMEM),
        ),
        out_shape=jax.ShapeDtypeStruct((chunks * per, size, rhs), jnp.bfloat16),
        compiler_params=params(),
        name="low_base",
    )(scalars, *zero)


def last_solve(own, other, inverse, solved, copies):
    count, size, rhs = own.shape

    def kernel(own_ref, other_ref, inverse_ref, solved_ref, out_ref):
        for h in range(count):
            value = (own_ref[h] + other_ref[h].astype(jnp.float32)).astype(jnp.bfloat16)
            value = jnp.dot(inverse_ref[h, 0], value, preferred_element_type=jnp.float32)
            value = (value + solved_ref[h].astype(jnp.float32)).astype(jnp.bfloat16)
            for copy in range(copies):
                out_ref[h * copies + copy] = value

    return pl.pallas_call(
        kernel,
        out_shape=jax.ShapeDtypeStruct((count * copies, size, rhs), jnp.bfloat16),
        compiler_params=params(),
        name="last_solve",
    )(own, other, inverse, solved)


def on_device(right_sides, factor, pattern, lower_inverse, upper_inverse):
    lo_n = lax.axis_size("lo")
    prow_n = lax.axis_size("hi") * lo_n
    q_n = lax.axis_size("q")
    pcol_n = q_n * lax.axis_size("s")
    row_id = lax.axis_index("hi") * lo_n + lax.axis_index("lo")
    q_id = lax.axis_index("q")
    s_id = lax.axis_index("s")
    col_id = q_id * prow_n + s_id
    row_blocks, _, col_blocks, _, size, _ = factor.shape
    rhs = right_sides.shape[1]
    per = right_sides.shape[0] // size
    spread_n = pcol_n // per
    half = row_blocks // 2
    bounds = (0, half, 3 * row_blocks // 4, 7 * row_blocks // 8, row_blocks)
    cols = tuple(q_n * b for b in bounds)
    device = lambda r, c: r * pcol_n + c
    everyone = [(r, c) for r in range(prow_n) for c in range(pcol_n)]

    is_low = row_id < prow_n // 2
    hi_id = lax.axis_index("hi")
    lo_id = lax.axis_index("lo")
    entries = [q_id, col_id, lo_id]
    scalars = jnp.stack([jnp.asarray(v, jnp.int32) for v in entries])
    pattern = pattern.reshape(row_blocks, col_blocks)
    first_low = half // per

    def route(t, r, c):
        q, s = divmod(c, prow_n)
        up, low = divmod(r, lo_n)
        if t == 0:
            return s, q * prow_n + (1 - up) * lo_n + low
        up = (up + 1 + s // lo_n + q) % 2
        return s, (q + t) % q_n * prow_n + up * lo_n + lo_n - 1 - low

    def spread(values):
        return [
            lax.ppermute(values, ALL_AXES, [(device(r, c), device(*route(t, r, c))) for r, c in everyone])
            for t in reversed(range(q_n))
        ][::-1]

    def spread_groups(first, last):
        def groups(scal):
            ids = [lax.rem(scal[0] + (q_n - t), q_n) if scal is not None else 0 for t in range(q_n)]
            return [q_n * m + q for q in ids for m in range(first, last, 2)]

        return groups

    def summands(partial):
        step = prow_n // 2
        while True:
            pairs = [(device(r, c), device(r ^ step, c)) for r, c in everyone]
            other = lax.ppermute(partial, ALL_AXES, pairs)
            step //= 2
            if step == 0:
                return [partial, other]
            partial = partial + other

    def count(level):
        return bounds[level + 1] - bounds[level]

    def part(level, groups, step):
        return (count(level), lambda scal: [bounds[level]], groups, step)

    def laid_out(after, *parts):
        return lay_out(scalars, pattern, factor, after, parts)

    low_starts = lambda scal: [per * lax.rem(scal[2] + t, lo_n) if scal is not None else 0 for t in range(lo_n)]
    low_rows = (half, low_starts)
    late_rows = (count(2) + count(3), lambda scal: [bounds[2]])

    if per == prow_n and lo_n == 2 and pcol_n & (pcol_n - 1) == 0:

        def chunk(r, c):
            q, s = c // prow_n, c % prow_n
            return (r // lo_n + s // lo_n + 1 + q) % 2 * lo_n + r % lo_n

        there = [(device(r, c), device(c % prow_n, chunk(r, c) * q_n + c // prow_n)) for r, c in everyone]
        back = [(target, source) for source, target in there]
        chunk_id = chunk(row_id, col_id)
        inverse_rows = lax.dynamic_index_in_dim(
            lower_inverse[:half].reshape(first_low, per, size, size), chunk_id, 1, keepdims=False
        )

        def zero_groups(scal):
            ids = [scal[1] ^ t if scal is not None else 0 for t in range(pcol_n)]
            return [c + pcol_n * r for c in ids for r in range(0, first_low, 2)]

        def exchange(values, t):
            return lax.ppermute(values, ALL_AXES, [(device(r, c), device(r, c ^ t)) for r, c in everyone])

        (one_zero,) = laid_out([inverse_rows], part(1, zero_groups, pcol_n))
        inverse_rows = lax.ppermute(inverse_rows, ALL_AXES, there)
        blocks = right_sides.reshape(2, 2, size, rhs)
        for axis, name, index in ((0, "hi", hi_id), (1, "lo", lo_id)):
            other = lax.dynamic_index_in_dim(blocks, 1 - index, axis, keepdims=False)
            other = lax.ppermute(other, name, [(0, 1), (1, 0)])
            own = lax.dynamic_index_in_dim(blocks, index, axis, keepdims=False)
            blocks = jnp.where(index == 0, jnp.stack([own, other], axis), jnp.stack([other, own], axis))
        blocks = blocks.reshape(per, size, rhs)
        rest = lax.ppermute(blocks[first_low:], ALL_AXES, back)
        own_zero = solve_blocks(inverse_rows, blocks[:first_low], [one_zero])
        even = {t: exchange(own_zero, t) for t in range(pcol_n - 2, 0, -2)}
        even[0] = own_zero
        zero = []
        for t in range(0, pcol_n, 2):
            zero += [even[t], exchange(even[t], 1)]
        zero_step = pcol_n

        owned = (jnp.arange(per) == chunk_id)[None, :, None, None]
        base = jnp.where(owned, rest[:, None], jnp.zeros((), jnp.bfloat16)).reshape(row_blocks - half, size, rhs)
        base_zero = low_base(scalars, zero, row_id == s_id, per, q_n, lo_n)
    else:
        group_rows = lax.all_gather(right_sides.reshape(per, size, rhs), COL_AXES, axis=0, tiled=True)
        picked = lax.dynamic_index_in_dim(group_rows.reshape(per, pcol_n, size, rhs), col_id, 1, keepdims=False)
        mine = lax.all_gather(picked, ROW_AXES, axis=0, tiled=True)
        own_zero = sum_and_solve([mine[:half]], [lower_inverse], 0)
        zero_groups = spread_groups(0, half)
        zero_step = q_n
        (one_zero,) = laid_out([own_zero], part(1, zero_groups, zero_step))
        zero = spread(own_zero)
        base = jnp.where(row_id == 0, mine[half:], jnp.zeros((), jnp.bfloat16))
        base_zero = jnp.where(row_id == 0, own_zero, jnp.zeros((), jnp.bfloat16))
        base_zero = lax.dynamic_slice_in_dim(jnp.concatenate([base_zero, base_zero]), per * lo_id, half, 0)

    level_groups = [zero_groups] + [spread_groups(bounds[level], bounds[level + 1]) for level in range(1, 4)]
    partial = block_sums([(one_zero, zero)], 0, count(1), None, (base, 0), True)
    one_rows = sum_and_solve(summands(partial), [lower_inverse], bounds[1])
    one = spread(one_rows)
    late_zero, two_one = laid_out([one_rows, base_zero], (*late_rows, zero_groups, zero_step), part(2, level_groups[1], q_n))
    late = block_sums([(late_zero, zero)], 0, count(2) + count(3), None, (base, bounds[2] - half), False)
    partial = block_sums([(two_one, one)], 0, count(2), (late, 0), None, True)
    two_rows = sum_and_solve(summands(partial), [lower_inverse], bounds[2])
    two = spread(two_rows)
    three_one, three_two = laid_out([two_rows], part(3, level_groups[1], q_n), part(3, level_groups[2], q_n))
    late = block_sums([(three_one, one)], 0, count(3), (late, count(2)), None, False)
    partial = block_sums([(three_two, two)], 0, count(3), (late, 0), None, True)
    three_solved = sum_and_solve(summands(partial), [lower_inverse, upper_inverse], bounds[3])
    three = spread(three_solved)
    two_three, one_three, one_two, zero_three = laid_out(
        [three_solved],
        part(2, level_groups[3], q_n),
        part(1, level_groups[3], q_n),
        part(1, level_groups[2], q_n),
        (*low_rows, level_groups[3], q_n),
    )
    partial = block_sums([(two_three, three)], 0, count(2), None, None, True)
    two_solved = sum_and_solve(summands(partial) + [two_rows], [upper_inverse], bounds[2])
    two = spread(two_solved)
    zero_two, zero_one = laid_out([two_solved], (*low_rows, level_groups[2], q_n), (*low_rows, level_groups[1], q_n))
    late = block_sums([(one_three, three)], 0, count(1), None, None, False)
    partial = block_sums([(one_two, two)], 0, count(1), (late, 0), None, True)
    one_solved = sum_and_solve(summands(partial) + [one_rows], [upper_inverse], bounds[1])
    one = spread(one_solved)
    upper = block_sums([(zero_three, three), (zero_two, two)], 0, half, None, (base_zero, 0), False)
    own, *chunks = low_sums(zero_one, one, upper, lo_n)
    own = own.astype(jnp.float32)
    for t in range(1, lo_n):
        pairs = [((lo, (lo + t) % lo_n)) for lo in range(lo_n)]
        own = own + lax.ppermute(chunks[t - 1], "lo", pairs).astype(jnp.float32)
    other = lax.ppermute(own.astype(jnp.bfloat16), "hi", [(0, 1), (1, 0)])
    solved = jnp.concatenate([one_solved, two_solved, three_solved], axis=0)
    solved = lax.dynamic_slice_in_dim(solved, per * lo_id, per, 0)
    last_inverse = lax.dynamic_slice_in_dim(upper_inverse, per * lo_id, per, 0)
    last_inverse = jnp.where(is_low, last_inverse, jnp.zeros((), jnp.bfloat16))
    solved = jnp.where(is_low, jnp.zeros((), jnp.bfloat16), solved)
    slots = last_solve(own, other, last_inverse, solved, spread_n)
    received = lax.all_to_all(slots, COL_AXES, 0, 0, tiled=True)
    mine = lax.dynamic_slice_in_dim(received, lax.rem(col_id, spread_n) * per, per, 0)
    return mine.reshape(per * size, rhs)


def solution(mesh):
    prow_n, pcol_n = mesh.shape["prow"], mesh.shape["pcol"]
    fine = Mesh(mesh.devices.reshape(2, prow_n // 2, pcol_n // prow_n, prow_n), ALL_AXES)
    placed = (
        P(ALL_AXES, None),
        P(None, COL_AXES, None, ROW_AXES, None, None),
        P(None, COL_AXES, None, ROW_AXES),
        P(None, COL_AXES, None, None),
        P(None, COL_AXES, None, None),
    )
    return jax.shard_map(on_device, mesh=fine, in_specs=placed, out_specs=P(ALL_AXES, None), check_vma=False)
```

```python
import math

import jax
import jax.numpy as jnp
from jax import lax
from jax.experimental import pallas as pl
from jax.experimental.pallas import tpu as pltpu
from jax.sharding import Mesh
from jax.sharding import PartitionSpec as P

ROW_AXES = ("hi", "lo")
COL_AXES = ("q", "s")
ALL_AXES = ROW_AXES + COL_AXES
VMEM_LIMIT = 16 * 1024 * 1024


def params():
    return pltpu.CompilerParams(vmem_limit_bytes=VMEM_LIMIT)


def lay_out(scalars, pattern, factor, after, parts):
    size = factor.shape[-1]
    shapes = [(len(groups(None)), rows, 2, size, size) for rows, _, groups, _ in parts]
    copy_count = sum(len(starts(None)) * len(groups(None)) for _, starts, groups, _ in parts)
    steps = sorted({step for _, _, _, step in parts})
    operands = [factor.reshape(factor.shape[0], -1, step, size, size) for step in steps]

    def kernel(scal, pat, *refs):
        factor_refs = dict(zip(steps, refs))
        out_refs = refs[len(steps) + len(after) : -1]
        sems = refs[-1]
        copies = []
        for (rows, starts, groups, step), out_ref in zip(parts, out_refs):
            run = rows // len(starts(scal))
            part_copies = []
            for g, column in enumerate(groups(scal)):
                for n, start in enumerate(starts(scal)):
                    place = sum(map(len, copies)) + len(part_copies)
                    part_copies.append(
                        pltpu.make_async_copy(
                            factor_refs[step].at[
                                pl.ds(start, run), pl.ds(column // step, 2), column % step
                            ],
                            out_ref.at[g, pl.ds(n * run, run)],
                            sems.at[place],
                        )
                    )
            for copy in part_copies:
                copy.start()
            copies.append(part_copies)
        for (rows, starts, groups, step), out_ref, part_copies in zip(parts, out_refs, copies):
            first_rows = starts(scal)
            run = rows // len(first_rows)
            for g, column in enumerate(groups(scal)):
                for n, start in enumerate(first_rows):
                    part_copies[g * len(first_rows) + n].wait()
                    for i in range(run):
                        for k in range(2):

                            @pl.when(pat[start + i, column + k * step] == 0)
                            def _(g=g, n=n, i=i, k=k, run=run, out_ref=out_ref):
                                out_ref[g, n * run + i, k] = jnp.zeros((size, size), jnp.bfloat16)

    return pl.pallas_call(
        kernel,
        grid_spec=pltpu.PrefetchScalarGridSpec(
            num_scalar_prefetch=2,
            grid=(1,),
            in_specs=[pl.BlockSpec(memory_space=pl.ANY)] * (len(steps) + len(after)),
            out_specs=[pl.BlockSpec(memory_space=pltpu.VMEM)] * len(parts),
            scratch_shapes=[pltpu.SemaphoreType.DMA((copy_count,))],
        ),
        out_shape=[jax.ShapeDtypeStruct(shape, jnp.bfloat16) for shape in shapes],
        compiler_params=params(),
        cost_estimate=pl.CostEstimate(
            flops=0, bytes_accessed=sum(8 * math.prod(shape) for shape in shapes), transcendentals=0
        ),
        name="lay_out",
    )(scalars, pattern, *[pltpu.with_memory_space_constraint(operand, pltpu.HBM) for operand in operands], *after)


def block_sums(parts, first_row, row_count, acc, base, negate):
    size, rhs = parts[0][1][0].shape[1:]
    rows = slice(first_row, first_row + row_count)

    def kernel(*refs):
        refs = list(refs)
        out_ref = refs.pop()
        total = jnp.zeros((row_count * size, rhs), jnp.float32)
        for blocks, values in parts:
            blocks_ref = refs.pop(0)
            place = 0
            for value in values:
                value_ref = refs.pop(0)
                for start in range(0, value.shape[0], 2):
                    right = value_ref[start : start + 2].reshape(2 * size, rhs)
                    left = jnp.concatenate([blocks_ref[place, rows, n] for n in range(2)], axis=2)
                    left = left.reshape(row_count * size, 2 * size)
                    total = total + jnp.dot(left, right, preferred_element_type=jnp.float32)
                    place += 1
        total = total.reshape(row_count, size, rhs)
        if acc is not None:
            total = total + refs.pop(0)[acc[1] : acc[1] + row_count]
        if base is not None:
            total = total - refs.pop(0)[base[1] : base[1] + row_count].astype(jnp.float32)
        out_ref[...] = (-total if negate else total).astype(out_ref.dtype)

    operands = []
    for blocks, values in parts:
        operands += [blocks, *values]
    operands += [extra[0] for extra in (acc, base) if extra is not None]
    blocks_used = 2 * row_count * sum(blocks.shape[0] for blocks, _ in parts)
    return pl.pallas_call(
        kernel,
        out_shape=jax.ShapeDtypeStruct((row_count, size, rhs), jnp.bfloat16 if negate else jnp.float32),
        compiler_params=params(),
        cost_estimate=pl.CostEstimate(
            flops=2 * blocks_used * size * size * rhs, bytes_accessed=2 * blocks_used * size * size, transcendentals=0
        ),
        name="block_sums",
    )(*operands)


def low_sums(blocks, values, acc, chunks):
    rows, size, rhs = acc.shape

    def kernel(blocks_ref, *refs):
        value_refs, acc_ref, out_refs = refs[: len(values)], refs[len(values)], refs[len(values) + 1 :]
        total = acc_ref[...].reshape(rows * size, rhs)
        place = 0
        for value, ref in zip(values, value_refs):
            for start in range(0, value.shape[0], 2):
                left = jnp.concatenate([blocks_ref[place, :, n] for n in range(2)], axis=2)
                right = ref[start : start + 2].reshape(2 * size, rhs)
                total = total + jnp.dot(
                    left.reshape(rows * size, 2 * size), right, preferred_element_type=jnp.float32
                )
                place += 1
        total = (-total).astype(jnp.bfloat16).reshape(chunks, rows // chunks, size, rhs)
        for n, ref in enumerate(out_refs):
            ref[...] = total[n]

    return pl.pallas_call(
        kernel,
        out_shape=[jax.ShapeDtypeStruct((rows // chunks, size, rhs), jnp.bfloat16)] * chunks,
        compiler_params=params(),
        name="low_sums",
    )(blocks, *values, acc)


def sum_and_solve(terms, inverses, row_start):
    rows, size, rhs = terms[0].shape
    term_count = len(terms)

    def kernel(*refs):
        term_refs = refs[:term_count]
        inverse_refs = refs[term_count:-1]
        for i in range(rows):
            value = term_refs[0][i].astype(jnp.float32)
            for ref in term_refs[1:]:
                value = value + ref[i].astype(jnp.float32)
            value = value.astype(jnp.bfloat16)
            for inverse_ref in inverse_refs:
                value = jnp.dot(inverse_ref[i, 0], value, preferred_element_type=jnp.float32).astype(jnp.bfloat16)
            refs[-1][i] = value

    whole = pl.BlockSpec((rows, size, rhs), lambda g: (0, 0, 0))
    inverse = pl.BlockSpec((rows, 1, size, size), lambda g: (row_start // rows, 0, 0, 0))
    return pl.pallas_call(
        kernel,
        grid=(1,),
        in_specs=[whole] * term_count + [inverse] * len(inverses),
        out_specs=whole,
        out_shape=jax.ShapeDtypeStruct((rows, size, rhs), jnp.bfloat16),
        compiler_params=params(),
        cost_estimate=pl.CostEstimate(
            flops=2 * rows * size * size * rhs, bytes_accessed=2 * (term_count + 2) * rows * size * rhs, transcendentals=0
        ),
        name="sum_and_solve",
    )(*terms, *inverses)


def solve_blocks(inverse, values, after):
    count, size, rhs = values.shape

    def kernel(inverse_ref, value_ref, *refs):
        out_ref = refs[-1]
        for i in range(count):
            out_ref[i] = jnp.dot(inverse_ref[i], value_ref[i], preferred_element_type=jnp.float32).astype(jnp.bfloat16)

    return pl.pallas_call(
        kernel,
        in_specs=[pl.BlockSpec(memory_space=pltpu.VMEM)] * 2 + [pl.BlockSpec(memory_space=pl.ANY)] * len(after),
        out_shape=jax.ShapeDtypeStruct(values.shape, jnp.bfloat16),
        compiler_params=params(),
        name="solve_blocks",
    )(inverse, values, *after)


def low_base(scalars, zero, keep, per, q_n, lo_n):
    chunks, size, rhs = zero[0].shape
    scalars = jnp.concatenate([scalars, keep[None].astype(jnp.int32)])

    def kernel(scal, *refs):
        out_ref = refs[-1]
        for h in range(per):
            source = scal[1] ^ (h * q_n + scal[0])
            for r in range(chunks):
                value = jnp.zeros((size, rhs), jnp.bfloat16)
                for t, ref in enumerate(refs[:-1]):
                    value = jnp.where((source == t) & (scal[3] > 0), ref[r], value)
                place = lax.rem(r + lo_n - scal[2], lo_n)
                out_ref[place * per + h] = value

    return pl.pallas_call(
        kernel,
        grid_spec=pltpu.PrefetchScalarGridSpec(
            num_scalar_prefetch=1,
            grid=(1,),
            in_specs=[pl.BlockSpec(memory_space=pltpu.VMEM)] * len(zero),
            out_specs=pl.BlockSpec(memory_space=pltpu.VMEM),
        ),
        out_shape=jax.ShapeDtypeStruct((chunks * per, size, rhs), jnp.bfloat16),
        compiler_params=params(),
        name="low_base",
    )(scalars, *zero)


def last_solve(own, other, inverse, solved, copies):
    count, size, rhs = own.shape

    def kernel(own_ref, other_ref, inverse_ref, solved_ref, out_ref):
        for h in range(count):
            value = (own_ref[h] + other_ref[h].astype(jnp.float32)).astype(jnp.bfloat16)
            value = jnp.dot(inverse_ref[h, 0], value, preferred_element_type=jnp.float32)
            value = (value + solved_ref[h].astype(jnp.float32)).astype(jnp.bfloat16)
            for copy in range(copies):
                out_ref[h * copies + copy] = value

    return pl.pallas_call(
        kernel,
        out_shape=jax.ShapeDtypeStruct((count * copies, size, rhs), jnp.bfloat16),
        compiler_params=params(),
        name="last_solve",
    )(own, other, inverse, solved)


def on_device(right_sides, factor, pattern, lower_inverse, upper_inverse):
    lo_n = lax.axis_size("lo")
    prow_n = lax.axis_size("hi") * lo_n
    q_n = lax.axis_size("q")
    pcol_n = q_n * lax.axis_size("s")
    row_id = lax.axis_index("hi") * lo_n + lax.axis_index("lo")
    q_id = lax.axis_index("q")
    s_id = lax.axis_index("s")
    col_id = q_id * prow_n + s_id
    row_blocks, _, col_blocks, _, size, _ = factor.shape
    rhs = right_sides.shape[1]
    per = right_sides.shape[0] // size
    spread_n = pcol_n // per
    half = row_blocks // 2
    bounds = (0, half, 3 * row_blocks // 4, 7 * row_blocks // 8, row_blocks)
    cols = tuple(q_n * b for b in bounds)
    device = lambda r, c: r * pcol_n + c
    everyone = [(r, c) for r in range(prow_n) for c in range(pcol_n)]

    is_low = row_id < prow_n // 2
    hi_id = lax.axis_index("hi")
    lo_id = lax.axis_index("lo")
    entries = [q_id, col_id, lo_id]
    scalars = jnp.stack([jnp.asarray(v, jnp.int32) for v in entries])
    pattern = pattern.reshape(row_blocks, col_blocks)
    first_low = half // per

    def route(t, r, c):
        q, s = divmod(c, prow_n)
        up, low = divmod(r, lo_n)
        if t == 0:
            return s, q * prow_n + (1 - up) * lo_n + low
        up = (up + 1 + s // lo_n + q) % 2
        return s, (q + t) % q_n * prow_n + up * lo_n + lo_n - 1 - low

    def spread(values):
        return [
            lax.ppermute(values, ALL_AXES, [(device(r, c), device(*route(t, r, c))) for r, c in everyone])
            for t in reversed(range(q_n))
        ][::-1]

    def spread_groups(first, last):
        def groups(scal):
            ids = [lax.rem(scal[0] + (q_n - t), q_n) if scal is not None else 0 for t in range(q_n)]
            return [q_n * m + q for q in ids for m in range(first, last, 2)]

        return groups

    def summands(partial):
        step = prow_n // 2
        while True:
            pairs = [(device(r, c), device(r ^ step, c)) for r, c in everyone]
            other = lax.ppermute(partial, ALL_AXES, pairs)
            step //= 2
            if step == 0:
                return [partial, other]
            partial = partial + other

    def count(level):
        return bounds[level + 1] - bounds[level]

    def part(level, groups, step):
        return (count(level), lambda scal: [bounds[level]], groups, step)

    def laid_out(after, *parts):
        return lay_out(scalars, pattern, factor, after, parts)

    low_starts = lambda scal: [per * lax.rem(scal[2] + t, lo_n) if scal is not None else 0 for t in range(lo_n)]
    low_rows = (half, low_starts)
    late_rows = (count(2) + count(3), lambda scal: [bounds[2]])

    if per == prow_n and lo_n == 2 and pcol_n & (pcol_n - 1) == 0:

        def chunk(r, c):
            q, s = c // prow_n, c % prow_n
            return (r // lo_n + s // lo_n + 1 + q) % 2 * lo_n + r % lo_n

        there = [(device(r, c), device(c % prow_n, chunk(r, c) * q_n + c // prow_n)) for r, c in everyone]
        back = [(target, source) for source, target in there]
        chunk_id = chunk(row_id, col_id)
        inverse_rows = lax.dynamic_index_in_dim(
            lower_inverse[:half].reshape(first_low, per, size, size), chunk_id, 1, keepdims=False
        )

        def zero_groups(scal):
            ids = [scal[1] ^ t if scal is not None else 0 for t in range(pcol_n)]
            return [c + pcol_n * r for c in ids for r in range(0, first_low, 2)]

        def exchange(values, t):
            return lax.ppermute(values, ALL_AXES, [(device(r, c), device(r, c ^ t)) for r, c in everyone])

        (one_zero,) = laid_out([inverse_rows], part(1, zero_groups, pcol_n))
        inverse_rows = lax.ppermute(inverse_rows, ALL_AXES, there)
        blocks = right_sides.reshape(2, 2, size, rhs)
        for axis, name, index in ((0, "hi", hi_id), (1, "lo", lo_id)):
            other = lax.dynamic_index_in_dim(blocks, 1 - index, axis, keepdims=False)
            other = lax.ppermute(other, name, [(0, 1), (1, 0)])
            own = lax.dynamic_index_in_dim(blocks, index, axis, keepdims=False)
            blocks = jnp.where(index == 0, jnp.stack([own, other], axis), jnp.stack([other, own], axis))
        blocks = blocks.reshape(per, size, rhs)
        rest = lax.ppermute(blocks[first_low:], ALL_AXES, back)
        own_zero = solve_blocks(inverse_rows, blocks[:first_low], [one_zero])
        even = {t: exchange(own_zero, t) for t in range(pcol_n - 2, 0, -2)}
        even[0] = own_zero
        zero = []
        for t in range(0, pcol_n, 2):
            zero += [even[t], exchange(even[t], 1)]
        zero_step = pcol_n

        owned = (jnp.arange(per) == chunk_id)[None, :, None, None]
        base = jnp.where(owned, rest[:, None], jnp.zeros((), jnp.bfloat16)).reshape(row_blocks - half, size, rhs)
        base_zero = low_base(scalars, zero, row_id == s_id, per, q_n, lo_n)
    else:
        group_rows = lax.all_gather(right_sides.reshape(per, size, rhs), COL_AXES, axis=0, tiled=True)
        picked = lax.dynamic_index_in_dim(group_rows.reshape(per, pcol_n, size, rhs), col_id, 1, keepdims=False)
        mine = lax.all_gather(picked, ROW_AXES, axis=0, tiled=True)
        own_zero = sum_and_solve([mine[:half]], [lower_inverse], 0)
        zero_groups = spread_groups(0, half)
        zero_step = q_n
        (one_zero,) = laid_out([own_zero], part(1, zero_groups, zero_step))
        zero = spread(own_zero)
        base = jnp.where(row_id == 0, mine[half:], jnp.zeros((), jnp.bfloat16))
        base_zero = jnp.where(row_id == 0, own_zero, jnp.zeros((), jnp.bfloat16))
        base_zero = lax.dynamic_slice_in_dim(jnp.concatenate([base_zero, base_zero]), per * lo_id, half, 0)

    level_groups = [zero_groups] + [spread_groups(bounds[level], bounds[level + 1]) for level in range(1, 4)]
    partial = block_sums([(one_zero, zero)], 0, count(1), None, (base, 0), True)
    one_rows = sum_and_solve(summands(partial), [lower_inverse], bounds[1])
    one = spread(one_rows)
    late_zero, two_one = laid_out([one_rows, base_zero], (*late_rows, zero_groups, zero_step), part(2, level_groups[1], q_n))
    late = block_sums([(late_zero, zero)], 0, count(2) + count(3), None, (base, bounds[2] - half), False)
    partial = block_sums([(two_one, one)], 0, count(2), (late, 0), None, True)
    two_rows = sum_and_solve(summands(partial), [lower_inverse], bounds[2])
    two = spread(two_rows)
    three_one, three_two = laid_out([two_rows], part(3, level_groups[1], q_n), part(3, level_groups[2], q_n))
    late = block_sums([(three_one, one)], 0, count(3), (late, count(2)), None, False)
    partial = block_sums([(three_two, two)], 0, count(3), (late, 0), None, True)
    three_solved = sum_and_solve(summands(partial), [lower_inverse, upper_inverse], bounds[3])
    three = spread(three_solved)
    two_three, one_three, one_two, zero_three = laid_out(
        [three_solved],
        part(2, level_groups[3], q_n),
        part(1, level_groups[3], q_n),
        part(1, level_groups[2], q_n),
        (*low_rows, level_groups[3], q_n),
    )
    partial = block_sums([(two_three, three)], 0, count(2), None, None, True)
    two_solved = sum_and_solve(summands(partial) + [two_rows], [upper_inverse], bounds[2])
    two = spread(two_solved)
    zero_two, zero_one = laid_out([two_solved], (*low_rows, level_groups[2], q_n), (*low_rows, level_groups[1], q_n))
    late = block_sums([(one_three, three)], 0, count(1), None, None, False)
    partial = block_sums([(one_two, two)], 0, count(1), (late, 0), None, True)
    one_solved = sum_and_solve(summands(partial) + [one_rows], [upper_inverse], bounds[1])
    one = spread(one_solved)
    upper = block_sums([(zero_three, three), (zero_two, two)], 0, half, None, (base_zero, 0), False)
    own, *chunks = low_sums(zero_one, one, upper, lo_n)
    own = own.astype(jnp.float32)
    for t in range(1, lo_n):
        pairs = [((lo, (lo + t) % lo_n)) for lo in range(lo_n)]
        own = own + lax.ppermute(chunks[t - 1], "lo", pairs).astype(jnp.float32)
    other = lax.ppermute(own.astype(jnp.bfloat16), "hi", [(0, 1), (1, 0)])
    solved = jnp.concatenate([one_solved, two_solved, three_solved], axis=0)
    solved = lax.dynamic_slice_in_dim(solved, per * lo_id, per, 0)
    last_inverse = lax.dynamic_slice_in_dim(upper_inverse, per * lo_id, per, 0)
    last_inverse = jnp.where(is_low, last_inverse, jnp.zeros((), jnp.bfloat16))
    solved = jnp.where(is_low, jnp.zeros((), jnp.bfloat16), solved)
    if spread_n == 2 and per & (per - 1) == 0:
        upper_id, last_id = col_id // 2, col_id % 2
        rows = last_solve(own, other, last_inverse, solved, 1)

        def pick(blocks, index):
            return lax.dynamic_index_in_dim(blocks, index, 0, keepdims=False)

        def crossed(values, t):
            return lax.ppermute(values, ALL_AXES, [(device(r, c), device(r, c ^ t)) for r, c in everyone])

        received = [crossed(pick(rows, upper_id ^ t), 2 * t) for t in range(per - 1, 0, -1)]
        received = jnp.stack([pick(rows, upper_id)] + received[::-1])
        kept, sent = [
            jnp.stack([pick(received, upper_id ^ (per // 2 * p + i)) for i in range(per // 2)])
            for p in (last_id, 1 - last_id)
        ]
        sent = crossed(sent, 1)
        mine = jnp.where(last_id == 0, jnp.stack([kept, sent], 1), jnp.stack([sent, kept], 1))
    else:
        slots = last_solve(own, other, last_inverse, solved, spread_n)
        received = lax.all_to_all(slots, COL_AXES, 0, 0, tiled=True)
        mine = lax.dynamic_slice_in_dim(received, lax.rem(col_id, spread_n) * per, per, 0)
    return mine.reshape(per * size, rhs)


def solution(mesh):
    prow_n, pcol_n = mesh.shape["prow"], mesh.shape["pcol"]
    fine = Mesh(mesh.devices.reshape(2, prow_n // 2, pcol_n // prow_n, prow_n), ALL_AXES)
    placed = (
        P(ALL_AXES, None),
        P(None, COL_AXES, None, ROW_AXES, None, None),
        P(None, COL_AXES, None, ROW_AXES),
        P(None, COL_AXES, None, None),
        P(None, COL_AXES, None, None),
    )
    return jax.shard_map(on_device, mesh=fine, in_specs=placed, out_specs=P(ALL_AXES, None), check_vma=False)
```

```python
import math

import jax
import jax.numpy as jnp
from jax import lax
from jax.experimental import pallas as pl
from jax.experimental.pallas import tpu as pltpu
from jax.sharding import Mesh
from jax.sharding import PartitionSpec as P

ROW_AXES = ("hi", "lo")
COL_AXES = ("q", "s")
ALL_AXES = ROW_AXES + COL_AXES
VMEM_LIMIT = 16 * 1024 * 1024


def params():
    return pltpu.CompilerParams(vmem_limit_bytes=VMEM_LIMIT)


def lay_out(scalars, pattern, factor, after, parts):
    size = factor.shape[-1]
    shapes = [(len(groups(None)), rows, 2, size, size) for rows, _, groups, _ in parts]
    copy_count = sum(len(starts(None)) * len(groups(None)) for _, starts, groups, _ in parts)
    steps = sorted({step for _, _, _, step in parts})
    operands = [factor.reshape(factor.shape[0], -1, step, size, size) for step in steps]

    def kernel(scal, pat, *refs):
        factor_refs = dict(zip(steps, refs))
        out_refs = refs[len(steps) + len(after) : -1]
        sems = refs[-1]
        copies = []
        for (rows, starts, groups, step), out_ref in zip(parts, out_refs):
            run = rows // len(starts(scal))
            part_copies = []
            for g, column in enumerate(groups(scal)):
                for n, start in enumerate(starts(scal)):
                    place = sum(map(len, copies)) + len(part_copies)
                    part_copies.append(
                        pltpu.make_async_copy(
                            factor_refs[step].at[
                                pl.ds(start, run), pl.ds(column // step, 2), column % step
                            ],
                            out_ref.at[g, pl.ds(n * run, run)],
                            sems.at[place],
                        )
                    )
            for copy in part_copies:
                copy.start()
            copies.append(part_copies)
        for (rows, starts, groups, step), out_ref, part_copies in zip(parts, out_refs, copies):
            first_rows = starts(scal)
            run = rows // len(first_rows)
            for g, column in enumerate(groups(scal)):
                for n, start in enumerate(first_rows):
                    part_copies[g * len(first_rows) + n].wait()
                    for i in range(run):
                        for k in range(2):

                            @pl.when(pat[start + i, column + k * step] == 0)
                            def _(g=g, n=n, i=i, k=k, run=run, out_ref=out_ref):
                                out_ref[g, n * run + i, k] = jnp.zeros((size, size), jnp.bfloat16)

    return pl.pallas_call(
        kernel,
        grid_spec=pltpu.PrefetchScalarGridSpec(
            num_scalar_prefetch=2,
            grid=(1,),
            in_specs=[pl.BlockSpec(memory_space=pl.ANY)] * (len(steps) + len(after)),
            out_specs=[pl.BlockSpec(memory_space=pltpu.VMEM)] * len(parts),
            scratch_shapes=[pltpu.SemaphoreType.DMA((copy_count,))],
        ),
        out_shape=[jax.ShapeDtypeStruct(shape, jnp.bfloat16) for shape in shapes],
        compiler_params=params(),
        cost_estimate=pl.CostEstimate(
            flops=0, bytes_accessed=sum(8 * math.prod(shape) for shape in shapes), transcendentals=0
        ),
        name="lay_out",
    )(scalars, pltpu.with_memory_space_constraint(pattern, pltpu.HBM), *[pltpu.with_memory_space_constraint(operand, pltpu.HBM) for operand in operands], *after)


def block_sums(parts, first_row, row_count, acc, base, negate):
    size, rhs = parts[0][1][0].shape[1:]
    rows = slice(first_row, first_row + row_count)

    def kernel(*refs):
        refs = list(refs)
        out_ref = refs.pop()
        total = jnp.zeros((row_count * size, rhs), jnp.float32)
        for blocks, values in parts:
            blocks_ref = refs.pop(0)
            place = 0
            for value in values:
                value_ref = refs.pop(0)
                for start in range(0, value.shape[0], 2):
                    right = value_ref[start : start + 2].reshape(2 * size, rhs)
                    left = jnp.concatenate([blocks_ref[place, rows, n] for n in range(2)], axis=2)
                    left = left.reshape(row_count * size, 2 * size)
                    total = total + jnp.dot(left, right, preferred_element_type=jnp.float32)
                    place += 1
        total = total.reshape(row_count, size, rhs)
        if acc is not None:
            total = total + refs.pop(0)[acc[1] : acc[1] + row_count]
        if base is not None:
            total = total - refs.pop(0)[base[1] : base[1] + row_count].astype(jnp.float32)
        out_ref[...] = (-total if negate else total).astype(out_ref.dtype)

    operands = []
    for blocks, values in parts:
        operands += [blocks, *values]
    operands += [extra[0] for extra in (acc, base) if extra is not None]
    blocks_used = 2 * row_count * sum(blocks.shape[0] for blocks, _ in parts)
    return pl.pallas_call(
        kernel,
        out_shape=jax.ShapeDtypeStruct((row_count, size, rhs), jnp.bfloat16 if negate else jnp.float32),
        compiler_params=params(),
        cost_estimate=pl.CostEstimate(
            flops=2 * blocks_used * size * size * rhs, bytes_accessed=2 * blocks_used * size * size, transcendentals=0
        ),
        name="block_sums",
    )(*operands)


def low_sums(blocks, values, acc, chunks):
    rows, size, rhs = acc.shape

    def kernel(blocks_ref, *refs):
        value_refs, acc_ref, out_refs = refs[: len(values)], refs[len(values)], refs[len(values) + 1 :]
        total = acc_ref[...].reshape(rows * size, rhs)
        place = 0
        for value, ref in zip(values, value_refs):
            for start in range(0, value.shape[0], 2):
                left = jnp.concatenate([blocks_ref[place, :, n] for n in range(2)], axis=2)
                right = ref[start : start + 2].reshape(2 * size, rhs)
                total = total + jnp.dot(
                    left.reshape(rows * size, 2 * size), right, preferred_element_type=jnp.float32
                )
                place += 1
        total = (-total).astype(jnp.bfloat16).reshape(chunks, rows // chunks, size, rhs)
        for n, ref in enumerate(out_refs):
            ref[...] = total[n]

    return pl.pallas_call(
        kernel,
        out_shape=[jax.ShapeDtypeStruct((rows // chunks, size, rhs), jnp.bfloat16)] * chunks,
        compiler_params=params(),
        name="low_sums",
    )(blocks, *values, acc)


def sum_and_solve(terms, inverses, row_start):
    rows, size, rhs = terms[0].shape
    term_count = len(terms)

    def kernel(*refs):
        term_refs = refs[:term_count]
        inverse_refs = refs[term_count:-1]
        for i in range(rows):
            value = term_refs[0][i].astype(jnp.float32)
            for ref in term_refs[1:]:
                value = value + ref[i].astype(jnp.float32)
            value = value.astype(jnp.bfloat16)
            for inverse_ref in inverse_refs:
                value = jnp.dot(inverse_ref[i, 0], value, preferred_element_type=jnp.float32).astype(jnp.bfloat16)
            refs[-1][i] = value

    whole = pl.BlockSpec((rows, size, rhs), lambda g: (0, 0, 0))
    inverse = pl.BlockSpec((rows, 1, size, size), lambda g: (row_start // rows, 0, 0, 0))
    return pl.pallas_call(
        kernel,
        grid=(1,),
        in_specs=[whole] * term_count + [inverse] * len(inverses),
        out_specs=whole,
        out_shape=jax.ShapeDtypeStruct((rows, size, rhs), jnp.bfloat16),
        compiler_params=params(),
        cost_estimate=pl.CostEstimate(
            flops=2 * rows * size * size * rhs, bytes_accessed=2 * (term_count + 2) * rows * size * rhs, transcendentals=0
        ),
        name="sum_and_solve",
    )(*terms, *inverses)


def solve_blocks(inverse, values, after):
    count, size, rhs = values.shape

    def kernel(inverse_ref, value_ref, *refs):
        out_ref = refs[-1]
        for i in range(count):
            out_ref[i] = jnp.dot(inverse_ref[i], value_ref[i], preferred_element_type=jnp.float32).astype(jnp.bfloat16)

    return pl.pallas_call(
        kernel,
        in_specs=[pl.BlockSpec(memory_space=pltpu.VMEM)] * 2 + [pl.BlockSpec(memory_space=pl.ANY)] * len(after),
        out_shape=jax.ShapeDtypeStruct(values.shape, jnp.bfloat16),
        compiler_params=params(),
        name="solve_blocks",
    )(inverse, values, *after)


def low_base(scalars, zero, keep, per, q_n, lo_n):
    chunks, size, rhs = zero[0].shape
    scalars = jnp.concatenate([scalars, keep[None].astype(jnp.int32)])

    def kernel(scal, *refs):
        out_ref = refs[-1]
        for h in range(per):
            source = scal[1] ^ (h * q_n + scal[0])
            for r in range(chunks):
                value = jnp.zeros((size, rhs), jnp.bfloat16)
                for t, ref in enumerate(refs[:-1]):
                    value = jnp.where((source == t) & (scal[3] > 0), ref[r], value)
                place = lax.rem(r + lo_n - scal[2], lo_n)
                out_ref[place * per + h] = value

    return pl.pallas_call(
        kernel,
        grid_spec=pltpu.PrefetchScalarGridSpec(
            num_scalar_prefetch=1,
            grid=(1,),
            in_specs=[pl.BlockSpec(memory_space=pltpu.VMEM)] * len(zero),
            out_specs=pl.BlockSpec(memory_space=pltpu.VMEM),
        ),
        out_shape=jax.ShapeDtypeStruct((chunks * per, size, rhs), jnp.bfloat16),
        compiler_params=params(),
        name="low_base",
    )(scalars, *zero)


def last_solve(own, other, inverse, solved, copies):
    count, size, rhs = own.shape

    def kernel(own_ref, other_ref, inverse_ref, solved_ref, out_ref):
        for h in range(count):
            value = (own_ref[h] + other_ref[h].astype(jnp.float32)).astype(jnp.bfloat16)
            value = jnp.dot(inverse_ref[h, 0], value, preferred_element_type=jnp.float32)
            value = (value + solved_ref[h].astype(jnp.float32)).astype(jnp.bfloat16)
            for copy in range(copies):
                out_ref[h * copies + copy] = value

    return pl.pallas_call(
        kernel,
        out_shape=jax.ShapeDtypeStruct((count * copies, size, rhs), jnp.bfloat16),
        compiler_params=params(),
        name="last_solve",
    )(own, other, inverse, solved)


def on_device(right_sides, factor, pattern, lower_inverse, upper_inverse):
    lo_n = lax.axis_size("lo")
    prow_n = lax.axis_size("hi") * lo_n
    q_n = lax.axis_size("q")
    pcol_n = q_n * lax.axis_size("s")
    row_id = lax.axis_index("hi") * lo_n + lax.axis_index("lo")
    q_id = lax.axis_index("q")
    s_id = lax.axis_index("s")
    col_id = q_id * prow_n + s_id
    row_blocks, _, col_blocks, _, size, _ = factor.shape
    rhs = right_sides.shape[1]
    per = right_sides.shape[0] // size
    spread_n = pcol_n // per
    half = row_blocks // 2
    bounds = (0, half, 3 * row_blocks // 4, 7 * row_blocks // 8, row_blocks)
    cols = tuple(q_n * b for b in bounds)
    device = lambda r, c: r * pcol_n + c
    everyone = [(r, c) for r in range(prow_n) for c in range(pcol_n)]

    is_low = row_id < prow_n // 2
    hi_id = lax.axis_index("hi")
    lo_id = lax.axis_index("lo")
    entries = [q_id, col_id, lo_id]
    scalars = jnp.stack([jnp.asarray(v, jnp.int32) for v in entries])
    pattern = pattern.reshape(row_blocks, col_blocks)
    first_low = half // per

    def route(t, r, c):
        q, s = divmod(c, prow_n)
        up, low = divmod(r, lo_n)
        if t == 0:
            return s, q * prow_n + (1 - up) * lo_n + low
        up = (up + 1 + s // lo_n + q) % 2
        return s, (q + t) % q_n * prow_n + up * lo_n + lo_n - 1 - low

    def spread(values):
        return [
            lax.ppermute(values, ALL_AXES, [(device(r, c), device(*route(t, r, c))) for r, c in everyone])
            for t in reversed(range(q_n))
        ][::-1]

    def spread_groups(first, last):
        def groups(scal):
            ids = [lax.rem(scal[0] + (q_n - t), q_n) if scal is not None else 0 for t in range(q_n)]
            return [q_n * m + q for q in ids for m in range(first, last, 2)]

        return groups

    def summands(partial):
        step = prow_n // 2
        while True:
            pairs = [(device(r, c), device(r ^ step, c)) for r, c in everyone]
            other = lax.ppermute(partial, ALL_AXES, pairs)
            step //= 2
            if step == 0:
                return [partial, other]
            partial = partial + other

    def count(level):
        return bounds[level + 1] - bounds[level]

    def part(level, groups, step):
        return (count(level), lambda scal: [bounds[level]], groups, step)

    def laid_out(after, *parts):
        return lay_out(scalars, pattern, factor, after, parts)

    low_starts = lambda scal: [per * lax.rem(scal[2] + t, lo_n) if scal is not None else 0 for t in range(lo_n)]
    low_rows = (half, low_starts)
    late_rows = (count(2) + count(3), lambda scal: [bounds[2]])

    if per == prow_n and lo_n == 2 and pcol_n & (pcol_n - 1) == 0:

        def chunk(r, c):
            q, s = c // prow_n, c % prow_n
            return (r // lo_n + s // lo_n + 1 + q) % 2 * lo_n + r % lo_n

        there = [(device(r, c), device(c % prow_n, chunk(r, c) * q_n + c // prow_n)) for r, c in everyone]
        back = [(target, source) for source, target in there]
        chunk_id = chunk(row_id, col_id)
        inverse_rows = lax.dynamic_index_in_dim(
            lower_inverse[:half].reshape(first_low, per, size, size), chunk_id, 1, keepdims=False
        )

        def zero_groups(scal):
            ids = [scal[1] ^ t if scal is not None else 0 for t in range(pcol_n)]
            return [c + pcol_n * r for c in ids for r in range(0, first_low, 2)]

        def exchange(values, t):
            return lax.ppermute(values, ALL_AXES, [(device(r, c), device(r, c ^ t)) for r, c in everyone])

        (one_zero,) = laid_out([inverse_rows], part(1, zero_groups, pcol_n))
        inverse_rows = lax.ppermute(inverse_rows, ALL_AXES, there)
        blocks = right_sides.reshape(2, 2, size, rhs)
        for axis, name, index in ((0, "hi", hi_id), (1, "lo", lo_id)):
            other = lax.dynamic_index_in_dim(blocks, 1 - index, axis, keepdims=False)
            other = lax.ppermute(other, name, [(0, 1), (1, 0)])
            own = lax.dynamic_index_in_dim(blocks, index, axis, keepdims=False)
            blocks = jnp.where(index == 0, jnp.stack([own, other], axis), jnp.stack([other, own], axis))
        blocks = blocks.reshape(per, size, rhs)
        own_zero = solve_blocks(inverse_rows, blocks[:first_low], [one_zero])
        even = {t: exchange(own_zero, t) for t in range(pcol_n - 2, 0, -2)}
        even[0] = own_zero
        zero = []
        for t in range(0, pcol_n, 2):
            zero += [even[t], exchange(even[t], 1)]
        rest = lax.ppermute(blocks[first_low:], ALL_AXES, back)
        zero_step = pcol_n

        owned = (jnp.arange(per) == chunk_id)[None, :, None, None]
        base = jnp.where(owned, rest[:, None], jnp.zeros((), jnp.bfloat16)).reshape(row_blocks - half, size, rhs)
        base_zero = low_base(scalars, zero, row_id == s_id, per, q_n, lo_n)
    else:
        group_rows = lax.all_gather(right_sides.reshape(per, size, rhs), COL_AXES, axis=0, tiled=True)
        picked = lax.dynamic_index_in_dim(group_rows.reshape(per, pcol_n, size, rhs), col_id, 1, keepdims=False)
        mine = lax.all_gather(picked, ROW_AXES, axis=0, tiled=True)
        own_zero = sum_and_solve([mine[:half]], [lower_inverse], 0)
        zero_groups = spread_groups(0, half)
        zero_step = q_n
        (one_zero,) = laid_out([own_zero], part(1, zero_groups, zero_step))
        zero = spread(own_zero)
        base = jnp.where(row_id == 0, mine[half:], jnp.zeros((), jnp.bfloat16))
        base_zero = jnp.where(row_id == 0, own_zero, jnp.zeros((), jnp.bfloat16))
        base_zero = lax.dynamic_slice_in_dim(jnp.concatenate([base_zero, base_zero]), per * lo_id, half, 0)

    level_groups = [zero_groups] + [spread_groups(bounds[level], bounds[level + 1]) for level in range(1, 4)]
    partial = block_sums([(one_zero, zero)], 0, count(1), None, (base, 0), True)
    one_rows = sum_and_solve(summands(partial), [lower_inverse], bounds[1])
    one = spread(one_rows)
    late_zero, two_one = laid_out([one_rows, base_zero], (*late_rows, zero_groups, zero_step), part(2, level_groups[1], q_n))
    late = block_sums([(late_zero, zero)], 0, count(2) + count(3), None, (base, bounds[2] - half), False)
    partial = block_sums([(two_one, one)], 0, count(2), (late, 0), None, True)
    two_rows = sum_and_solve(summands(partial), [lower_inverse], bounds[2])
    two = spread(two_rows)
    three_one, three_two = laid_out([two_rows], part(3, level_groups[1], q_n), part(3, level_groups[2], q_n))
    late = block_sums([(three_one, one)], 0, count(3), (late, count(2)), None, False)
    partial = block_sums([(three_two, two)], 0, count(3), (late, 0), None, True)
    three_solved = sum_and_solve(summands(partial), [lower_inverse, upper_inverse], bounds[3])
    three = spread(three_solved)
    two_three, one_three, one_two, zero_three = laid_out(
        [three_solved],
        part(2, level_groups[3], q_n),
        part(1, level_groups[3], q_n),
        part(1, level_groups[2], q_n),
        (*low_rows, level_groups[3], q_n),
    )
    partial = block_sums([(two_three, three)], 0, count(2), None, None, True)
    two_solved = sum_and_solve(summands(partial) + [two_rows], [upper_inverse], bounds[2])
    two = spread(two_solved)
    zero_two, zero_one = laid_out([two_solved], (*low_rows, level_groups[2], q_n), (*low_rows, level_groups[1], q_n))
    late = block_sums([(one_three, three)], 0, count(1), None, None, False)
    partial = block_sums([(one_two, two)], 0, count(1), (late, 0), None, True)
    one_solved = sum_and_solve(summands(partial) + [one_rows], [upper_inverse], bounds[1])
    one = spread(one_solved)
    upper = block_sums([(zero_three, three), (zero_two, two)], 0, half, None, (base_zero, 0), False)
    own, *chunks = low_sums(zero_one, one, upper, lo_n)
    own = own.astype(jnp.float32)
    for t in range(1, lo_n):
        pairs = [((lo, (lo + t) % lo_n)) for lo in range(lo_n)]
        own = own + lax.ppermute(chunks[t - 1], "lo", pairs).astype(jnp.float32)
    other = lax.ppermute(own.astype(jnp.bfloat16), "hi", [(0, 1), (1, 0)])
    solved = jnp.concatenate([one_solved, two_solved, three_solved], axis=0)
    solved = lax.dynamic_slice_in_dim(solved, per * lo_id, per, 0)
    last_inverse = lax.dynamic_slice_in_dim(upper_inverse, per * lo_id, per, 0)
    last_inverse = jnp.where(is_low, last_inverse, jnp.zeros((), jnp.bfloat16))
    solved = jnp.where(is_low, jnp.zeros((), jnp.bfloat16), solved)
    if spread_n == 2 and per & (per - 1) == 0:
        upper_id, last_id = col_id // 2, col_id % 2
        rows = last_solve(own, other, last_inverse, solved, 1)

        def pick(blocks, index):
            return lax.dynamic_index_in_dim(blocks, index, 0, keepdims=False)

        def crossed(values, t):
            return lax.ppermute(values, ALL_AXES, [(device(r, c), device(r, c ^ t)) for r, c in everyone])

        received = [crossed(pick(rows, upper_id ^ t), 2 * t) for t in range(per - 1, 0, -1)]
        received = jnp.stack([pick(rows, upper_id)] + received[::-1])
        kept, sent = [
            jnp.stack([pick(received, upper_id ^ (per // 2 * p + i)) for i in range(per // 2)])
            for p in (last_id, 1 - last_id)
        ]
        sent = crossed(sent, 1)
        mine = jnp.where(last_id == 0, jnp.stack([kept, sent], 1), jnp.stack([sent, kept], 1))
    else:
        slots = last_solve(own, other, last_inverse, solved, spread_n)
        received = lax.all_to_all(slots, COL_AXES, 0, 0, tiled=True)
        mine = lax.dynamic_slice_in_dim(received, lax.rem(col_id, spread_n) * per, per, 0)
    return mine.reshape(per * size, rhs)


def solution(mesh):
    prow_n, pcol_n = mesh.shape["prow"], mesh.shape["pcol"]
    fine = Mesh(mesh.devices.reshape(2, prow_n // 2, pcol_n // prow_n, prow_n), ALL_AXES)
    placed = (
        P(ALL_AXES, None),
        P(None, COL_AXES, None, ROW_AXES, None, None),
        P(None, COL_AXES, None, ROW_AXES),
        P(None, COL_AXES, None, None),
        P(None, COL_AXES, None, None),
    )
    return jax.shard_map(on_device, mesh=fine, in_specs=placed, out_specs=P(ALL_AXES, None), check_vma=False)
```

```python
import math

import jax
import jax.numpy as jnp
from jax import lax
from jax.experimental import pallas as pl
from jax.experimental.pallas import tpu as pltpu
from jax.sharding import Mesh
from jax.sharding import PartitionSpec as P

ROW_AXES = ("hi", "lo")
COL_AXES = ("q", "s")
ALL_AXES = ROW_AXES + COL_AXES
VMEM_LIMIT = 16 * 1024 * 1024


def params():
    return pltpu.CompilerParams(vmem_limit_bytes=VMEM_LIMIT)


def lay_out(scalars, pattern, factor, after, parts):
    size = factor.shape[-1]
    shapes = [(len(groups(None)), rows, 2, size, size) for rows, _, groups, _ in parts]
    copy_count = sum(len(starts(None)) * len(groups(None)) for _, starts, groups, _ in parts)
    steps = sorted({step for _, _, _, step in parts})
    operands = [factor.reshape(factor.shape[0], -1, step, size, size) for step in steps]

    def kernel(scal, pat, *refs):
        factor_refs = dict(zip(steps, refs))
        out_refs = refs[len(steps) + len(after) : -1]
        sems = refs[-1]
        copies = []
        for (rows, starts, groups, step), out_ref in zip(parts, out_refs):
            run = rows // len(starts(scal))
            part_copies = []
            for g, column in enumerate(groups(scal)):
                for n, start in enumerate(starts(scal)):
                    place = sum(map(len, copies)) + len(part_copies)
                    part_copies.append(
                        pltpu.make_async_copy(
                            factor_refs[step].at[
                                pl.ds(start, run), pl.ds(column // step, 2), column % step
                            ],
                            out_ref.at[g, pl.ds(n * run, run)],
                            sems.at[place],
                        )
                    )
            for copy in part_copies:
                copy.start()
            copies.append(part_copies)
        for (rows, starts, groups, step), out_ref, part_copies in zip(parts, out_refs, copies):
            first_rows = starts(scal)
            run = rows // len(first_rows)
            for g, column in enumerate(groups(scal)):
                for n, start in enumerate(first_rows):
                    part_copies[g * len(first_rows) + n].wait()
                    for i in range(run):
                        for k in range(2):

                            @pl.when(pat[start + i, column + k * step] == 0)
                            def _(g=g, n=n, i=i, k=k, run=run, out_ref=out_ref):
                                out_ref[g, n * run + i, k] = jnp.zeros((size, size), jnp.bfloat16)

    return pl.pallas_call(
        kernel,
        grid_spec=pltpu.PrefetchScalarGridSpec(
            num_scalar_prefetch=2,
            grid=(1,),
            in_specs=[pl.BlockSpec(memory_space=pl.ANY)] * (len(steps) + len(after)),
            out_specs=[pl.BlockSpec(memory_space=pltpu.VMEM)] * len(parts),
            scratch_shapes=[pltpu.SemaphoreType.DMA((copy_count,))],
        ),
        out_shape=[jax.ShapeDtypeStruct(shape, jnp.bfloat16) for shape in shapes],
        compiler_params=params(),
        cost_estimate=pl.CostEstimate(
            flops=0, bytes_accessed=sum(8 * math.prod(shape) for shape in shapes), transcendentals=0
        ),
        name="lay_out",
    )(scalars, pltpu.with_memory_space_constraint(pattern, pltpu.HBM), *[pltpu.with_memory_space_constraint(operand, pltpu.HBM) for operand in operands], *after)


def block_sums(parts, first_row, row_count, acc, base, negate):
    size, rhs = parts[0][1][0].shape[1:]
    rows = slice(first_row, first_row + row_count)

    def kernel(*refs):
        refs = list(refs)
        out_ref = refs.pop()
        total = jnp.zeros((row_count * size, rhs), jnp.float32)
        for blocks, values in parts:
            blocks_ref = refs.pop(0)
            place = 0
            for value in values:
                value_ref = refs.pop(0)
                for start in range(0, value.shape[0], 2):
                    right = value_ref[start : start + 2].reshape(2 * size, rhs)
                    left = jnp.concatenate([blocks_ref[place, rows, n] for n in range(2)], axis=2)
                    left = left.reshape(row_count * size, 2 * size)
                    total = total + jnp.dot(left, right, preferred_element_type=jnp.float32)
                    place += 1
        total = total.reshape(row_count, size, rhs)
        if acc is not None:
            total = total + refs.pop(0)[acc[1] : acc[1] + row_count]
        if base is not None:
            total = total - refs.pop(0)[base[1] : base[1] + row_count].astype(jnp.float32)
        out_ref[...] = (-total if negate else total).astype(out_ref.dtype)

    operands = []
    for blocks, values in parts:
        operands += [blocks, *values]
    operands += [extra[0] for extra in (acc, base) if extra is not None]
    blocks_used = 2 * row_count * sum(blocks.shape[0] for blocks, _ in parts)
    return pl.pallas_call(
        kernel,
        out_shape=jax.ShapeDtypeStruct((row_count, size, rhs), jnp.bfloat16 if negate else jnp.float32),
        compiler_params=params(),
        cost_estimate=pl.CostEstimate(
            flops=2 * blocks_used * size * size * rhs, bytes_accessed=2 * blocks_used * size * size, transcendentals=0
        ),
        name="block_sums",
    )(*operands)


def low_sums(blocks, values, acc, chunks):
    rows, size, rhs = acc.shape

    def kernel(blocks_ref, *refs):
        value_refs, acc_ref, out_refs = refs[: len(values)], refs[len(values)], refs[len(values) + 1 :]
        total = acc_ref[...].reshape(rows * size, rhs)
        place = 0
        for value, ref in zip(values, value_refs):
            for start in range(0, value.shape[0], 2):
                left = jnp.concatenate([blocks_ref[place, :, n] for n in range(2)], axis=2)
                right = ref[start : start + 2].reshape(2 * size, rhs)
                total = total + jnp.dot(
                    left.reshape(rows * size, 2 * size), right, preferred_element_type=jnp.float32
                )
                place += 1
        total = (-total).astype(jnp.bfloat16).reshape(chunks, rows // chunks, size, rhs)
        for n, ref in enumerate(out_refs):
            ref[...] = total[n]

    return pl.pallas_call(
        kernel,
        out_shape=[jax.ShapeDtypeStruct((rows // chunks, size, rhs), jnp.bfloat16)] * chunks,
        compiler_params=params(),
        name="low_sums",
    )(blocks, *values, acc)


def sum_and_solve(terms, inverses, row_start):
    rows, size, rhs = terms[0].shape
    term_count = len(terms)

    def kernel(*refs):
        term_refs = refs[:term_count]
        inverse_refs = refs[term_count:-1]
        for i in range(rows):
            value = term_refs[0][i].astype(jnp.float32)
            for ref in term_refs[1:]:
                value = value + ref[i].astype(jnp.float32)
            value = value.astype(jnp.bfloat16)
            for inverse_ref in inverse_refs:
                value = jnp.dot(inverse_ref[i, 0], value, preferred_element_type=jnp.float32).astype(jnp.bfloat16)
            refs[-1][i] = value

    whole = pl.BlockSpec((rows, size, rhs), lambda g: (0, 0, 0))
    inverse = pl.BlockSpec((rows, 1, size, size), lambda g: (row_start // rows, 0, 0, 0))
    return pl.pallas_call(
        kernel,
        grid=(1,),
        in_specs=[whole] * term_count + [inverse] * len(inverses),
        out_specs=whole,
        out_shape=jax.ShapeDtypeStruct((rows, size, rhs), jnp.bfloat16),
        compiler_params=params(),
        cost_estimate=pl.CostEstimate(
            flops=2 * rows * size * size * rhs, bytes_accessed=2 * (term_count + 2) * rows * size * rhs, transcendentals=0
        ),
        name="sum_and_solve",
    )(*terms, *inverses)


def solve_blocks(inverse, values, after):
    count, size, rhs = values.shape

    def kernel(inverse_ref, value_ref, *refs):
        out_ref = refs[-1]
        for i in range(count):
            out_ref[i] = jnp.dot(inverse_ref[i], value_ref[i], preferred_element_type=jnp.float32).astype(jnp.bfloat16)

    return pl.pallas_call(
        kernel,
        in_specs=[pl.BlockSpec(memory_space=pltpu.VMEM)] * 2 + [pl.BlockSpec(memory_space=pl.ANY)] * len(after),
        out_shape=jax.ShapeDtypeStruct(values.shape, jnp.bfloat16),
        compiler_params=params(),
        name="solve_blocks",
    )(inverse, values, *after)


def low_base(scalars, zero, keep, per, q_n, lo_n):
    chunks, size, rhs = zero[0].shape
    scalars = jnp.concatenate([scalars, keep[None].astype(jnp.int32)])

    def kernel(scal, *refs):
        out_ref = refs[-1]
        for h in range(per):
            source = scal[1] ^ (h * q_n + scal[0])
            for r in range(chunks):
                value = jnp.zeros((size, rhs), jnp.bfloat16)
                for t, ref in enumerate(refs[:-1]):
                    value = jnp.where((source == t) & (scal[3] > 0), ref[r], value)
                place = lax.rem(r + lo_n - scal[2], lo_n)
                out_ref[place * per + h] = value

    return pl.pallas_call(
        kernel,
        grid_spec=pltpu.PrefetchScalarGridSpec(
            num_scalar_prefetch=1,
            grid=(1,),
            in_specs=[pl.BlockSpec(memory_space=pltpu.VMEM)] * len(zero),
            out_specs=pl.BlockSpec(memory_space=pltpu.VMEM),
        ),
        out_shape=jax.ShapeDtypeStruct((chunks * per, size, rhs), jnp.bfloat16),
        compiler_params=params(),
        name="low_base",
    )(scalars, *zero)


def last_solve(own, other, inverse, solved, copies):
    count, size, rhs = own.shape

    def kernel(own_ref, other_ref, inverse_ref, solved_ref, out_ref):
        for h in range(count):
            value = (own_ref[h] + other_ref[h].astype(jnp.float32)).astype(jnp.bfloat16)
            value = jnp.dot(inverse_ref[h, 0], value, preferred_element_type=jnp.float32)
            value = (value + solved_ref[h].astype(jnp.float32)).astype(jnp.bfloat16)
            for copy in range(copies):
                out_ref[h * copies + copy] = value

    return pl.pallas_call(
        kernel,
        out_shape=jax.ShapeDtypeStruct((count * copies, size, rhs), jnp.bfloat16),
        compiler_params=params(),
        name="last_solve",
    )(own, other, inverse, solved)


def on_device(right_sides, factor, pattern, lower_inverse, upper_inverse):
    lo_n = lax.axis_size("lo")
    prow_n = lax.axis_size("hi") * lo_n
    q_n = lax.axis_size("q")
    pcol_n = q_n * lax.axis_size("s")
    row_id = lax.axis_index("hi") * lo_n + lax.axis_index("lo")
    q_id = lax.axis_index("q")
    s_id = lax.axis_index("s")
    col_id = q_id * prow_n + s_id
    row_blocks, _, col_blocks, _, size, _ = factor.shape
    rhs = right_sides.shape[1]
    per = right_sides.shape[0] // size
    spread_n = pcol_n // per
    half = row_blocks // 2
    bounds = (0, half, 3 * row_blocks // 4, 7 * row_blocks // 8, row_blocks)
    cols = tuple(q_n * b for b in bounds)
    device = lambda r, c: r * pcol_n + c
    everyone = [(r, c) for r in range(prow_n) for c in range(pcol_n)]

    is_low = row_id < prow_n // 2
    hi_id = lax.axis_index("hi")
    lo_id = lax.axis_index("lo")
    entries = [q_id, col_id, lo_id]
    scalars = jnp.stack([jnp.asarray(v, jnp.int32) for v in entries])
    pattern = pattern.reshape(row_blocks, col_blocks)
    first_low = half // per

    def route(t, r, c):
        q, s = divmod(c, prow_n)
        up, low = divmod(r, lo_n)
        if t == 0:
            return s, q * prow_n + (1 - up) * lo_n + low
        up = (up + 1 + s // lo_n + q) % 2
        return s, (q + t) % q_n * prow_n + up * lo_n + lo_n - 1 - low

    def spread(values):
        return [
            lax.ppermute(values, ALL_AXES, [(device(r, c), device(*route(t, r, c))) for r, c in everyone])
            for t in reversed(range(q_n))
        ][::-1]

    def spread_groups(first, last):
        def groups(scal):
            ids = [lax.rem(scal[0] + (q_n - t), q_n) if scal is not None else 0 for t in range(q_n)]
            return [q_n * m + q for q in ids for m in range(first, last, 2)]

        return groups

    def summands(partial):
        step = prow_n // 2
        while True:
            pairs = [(device(r, c), device(r ^ step, c)) for r, c in everyone]
            other = lax.ppermute(partial, ALL_AXES, pairs)
            step //= 2
            if step == 0:
                return [partial, other]
            partial = partial + other

    def count(level):
        return bounds[level + 1] - bounds[level]

    def part(level, groups, step):
        return (count(level), lambda scal: [bounds[level]], groups, step)

    def laid_out(after, *parts):
        return lay_out(scalars, pattern, factor, after, parts)

    low_starts = lambda scal: [per * lax.rem(scal[2] + t, lo_n) if scal is not None else 0 for t in range(lo_n)]
    low_rows = (half, low_starts)
    late_rows = (count(2) + count(3), lambda scal: [bounds[2]])

    if per == prow_n and lo_n == 2 and pcol_n & (pcol_n - 1) == 0:

        def chunk(r, c):
            q, s = c // prow_n, c % prow_n
            return (r // lo_n + s // lo_n + 1 + q) % 2 * lo_n + r % lo_n

        there = [(device(r, c), device(c % prow_n, chunk(r, c) * q_n + c // prow_n)) for r, c in everyone]
        back = [(target, source) for source, target in there]
        chunk_id = chunk(row_id, col_id)
        inverse_rows = lax.dynamic_index_in_dim(
            lower_inverse[:half].reshape(first_low, per, size, size), chunk_id, 1, keepdims=False
        )

        def zero_groups(scal):
            ids = [scal[1] ^ t if scal is not None else 0 for t in range(pcol_n)]
            return [c + pcol_n * r for c in ids for r in range(0, first_low, 2)]

        def exchange(values, t):
            return lax.ppermute(values, ALL_AXES, [(device(r, c), device(r, c ^ t)) for r, c in everyone])

        (first_zero,) = laid_out([inverse_rows], part(1, lambda scal: zero_groups(scal)[:2], pcol_n))
        inverse_rows = lax.ppermute(inverse_rows, ALL_AXES, there)
        blocks = right_sides.reshape(2, 2, size, rhs)
        for axis, name, index in ((0, "hi", hi_id), (1, "lo", lo_id)):
            other = lax.dynamic_index_in_dim(blocks, 1 - index, axis, keepdims=False)
            other = lax.ppermute(other, name, [(0, 1), (1, 0)])
            own = lax.dynamic_index_in_dim(blocks, index, axis, keepdims=False)
            blocks = jnp.where(index == 0, jnp.stack([own, other], axis), jnp.stack([other, own], axis))
        blocks = blocks.reshape(per, size, rhs)
        own_zero = solve_blocks(inverse_rows, blocks[:first_low], [first_zero])
        (rest_zero,) = laid_out([own_zero], part(1, lambda scal: zero_groups(scal)[2:], pcol_n))
        even = {t: exchange(own_zero, t) for t in range(pcol_n - 2, 0, -2)}
        even[0] = own_zero
        zero = []
        for t in range(0, pcol_n, 2):
            zero += [even[t], exchange(even[t], 1)]
        rest = lax.ppermute(blocks[first_low:], ALL_AXES, back)
        one_zero = [(first_zero, zero[:2]), (rest_zero, zero[2:])]
        zero_step = pcol_n

        owned = (jnp.arange(per) == chunk_id)[None, :, None, None]
        base = jnp.where(owned, rest[:, None], jnp.zeros((), jnp.bfloat16)).reshape(row_blocks - half, size, rhs)
        base_zero = low_base(scalars, zero, row_id == s_id, per, q_n, lo_n)
    else:
        group_rows = lax.all_gather(right_sides.reshape(per, size, rhs), COL_AXES, axis=0, tiled=True)
        picked = lax.dynamic_index_in_dim(group_rows.reshape(per, pcol_n, size, rhs), col_id, 1, keepdims=False)
        mine = lax.all_gather(picked, ROW_AXES, axis=0, tiled=True)
        own_zero = sum_and_solve([mine[:half]], [lower_inverse], 0)
        zero_groups = spread_groups(0, half)
        zero_step = q_n
        (one_zero,) = laid_out([own_zero], part(1, zero_groups, zero_step))
        zero = spread(own_zero)
        one_zero = [(one_zero, zero)]
        base = jnp.where(row_id == 0, mine[half:], jnp.zeros((), jnp.bfloat16))
        base_zero = jnp.where(row_id == 0, own_zero, jnp.zeros((), jnp.bfloat16))
        base_zero = lax.dynamic_slice_in_dim(jnp.concatenate([base_zero, base_zero]), per * lo_id, half, 0)

    level_groups = [zero_groups] + [spread_groups(bounds[level], bounds[level + 1]) for level in range(1, 4)]
    partial = block_sums(one_zero, 0, count(1), None, (base, 0), True)
    one_rows = sum_and_solve(summands(partial), [lower_inverse], bounds[1])
    one = spread(one_rows)
    late_zero, two_one = laid_out([one_rows, base_zero], (*late_rows, zero_groups, zero_step), part(2, level_groups[1], q_n))
    late = block_sums([(late_zero, zero)], 0, count(2) + count(3), None, (base, bounds[2] - half), False)
    partial = block_sums([(two_one, one)], 0, count(2), (late, 0), None, True)
    two_rows = sum_and_solve(summands(partial), [lower_inverse], bounds[2])
    two = spread(two_rows)
    three_one, three_two = laid_out([two_rows], part(3, level_groups[1], q_n), part(3, level_groups[2], q_n))
    late = block_sums([(three_one, one)], 0, count(3), (late, count(2)), None, False)
    partial = block_sums([(three_two, two)], 0, count(3), (late, 0), None, True)
    three_solved = sum_and_solve(summands(partial), [lower_inverse, upper_inverse], bounds[3])
    three = spread(three_solved)
    two_three, one_three, one_two, zero_three = laid_out(
        [three_solved],
        part(2, level_groups[3], q_n),
        part(1, level_groups[3], q_n),
        part(1, level_groups[2], q_n),
        (*low_rows, level_groups[3], q_n),
    )
    partial = block_sums([(two_three, three)], 0, count(2), None, None, True)
    two_solved = sum_and_solve(summands(partial) + [two_rows], [upper_inverse], bounds[2])
    two = spread(two_solved)
    zero_two, zero_one = laid_out([two_solved], (*low_rows, level_groups[2], q_n), (*low_rows, level_groups[1], q_n))
    late = block_sums([(one_three, three)], 0, count(1), None, None, False)
    partial = block_sums([(one_two, two)], 0, count(1), (late, 0), None, True)
    one_solved = sum_and_solve(summands(partial) + [one_rows], [upper_inverse], bounds[1])
    one = spread(one_solved)
    upper = block_sums([(zero_three, three), (zero_two, two)], 0, half, None, (base_zero, 0), False)
    own, *chunks = low_sums(zero_one, one, upper, lo_n)
    own = own.astype(jnp.float32)
    for t in range(1, lo_n):
        pairs = [((lo, (lo + t) % lo_n)) for lo in range(lo_n)]
        own = own + lax.ppermute(chunks[t - 1], "lo", pairs).astype(jnp.float32)
    other = lax.ppermute(own.astype(jnp.bfloat16), "hi", [(0, 1), (1, 0)])
    solved = jnp.concatenate([one_solved, two_solved, three_solved], axis=0)
    solved = lax.dynamic_slice_in_dim(solved, per * lo_id, per, 0)
    last_inverse = lax.dynamic_slice_in_dim(upper_inverse, per * lo_id, per, 0)
    last_inverse = jnp.where(is_low, last_inverse, jnp.zeros((), jnp.bfloat16))
    solved = jnp.where(is_low, jnp.zeros((), jnp.bfloat16), solved)
    if spread_n == 2 and per & (per - 1) == 0:
        upper_id, last_id = col_id // 2, col_id % 2
        rows = last_solve(own, other, last_inverse, solved, 1)

        def pick(blocks, index):
            return lax.dynamic_index_in_dim(blocks, index, 0, keepdims=False)

        def crossed(values, t):
            return lax.ppermute(values, ALL_AXES, [(device(r, c), device(r, c ^ t)) for r, c in everyone])

        received = [crossed(pick(rows, upper_id ^ t), 2 * t) for t in range(per - 1, 0, -1)]
        received = jnp.stack([pick(rows, upper_id)] + received[::-1])
        kept, sent = [
            jnp.stack([pick(received, upper_id ^ (per // 2 * p + i)) for i in range(per // 2)])
            for p in (last_id, 1 - last_id)
        ]
        sent = crossed(sent, 1)
        mine = jnp.where(last_id == 0, jnp.stack([kept, sent], 1), jnp.stack([sent, kept], 1))
    else:
        slots = last_solve(own, other, last_inverse, solved, spread_n)
        received = lax.all_to_all(slots, COL_AXES, 0, 0, tiled=True)
        mine = lax.dynamic_slice_in_dim(received, lax.rem(col_id, spread_n) * per, per, 0)
    return mine.reshape(per * size, rhs)


def solution(mesh):
    prow_n, pcol_n = mesh.shape["prow"], mesh.shape["pcol"]
    fine = Mesh(mesh.devices.reshape(2, prow_n // 2, pcol_n // prow_n, prow_n), ALL_AXES)
    placed = (
        P(ALL_AXES, None),
        P(None, COL_AXES, None, ROW_AXES, None, None),
        P(None, COL_AXES, None, ROW_AXES),
        P(None, COL_AXES, None, None),
        P(None, COL_AXES, None, None),
    )
    return jax.shard_map(on_device, mesh=fine, in_specs=placed, out_specs=P(ALL_AXES, None), check_vma=False)
```

```python
import math

import jax
import jax.numpy as jnp
from jax import lax
from jax.experimental import pallas as pl
from jax.experimental.pallas import tpu as pltpu
from jax.sharding import Mesh
from jax.sharding import PartitionSpec as P

ROW_AXES = ("hi", "lo")
COL_AXES = ("q", "s")
ALL_AXES = ROW_AXES + COL_AXES
VMEM_LIMIT = 16 * 1024 * 1024


def params():
    return pltpu.CompilerParams(vmem_limit_bytes=VMEM_LIMIT)


def lay_out(scalars, pattern, factor, after, parts):
    size = factor.shape[-1]
    shapes = [(len(groups(None)), rows, 2, size, size) for rows, _, groups, _ in parts]
    copy_count = sum(len(starts(None)) * len(groups(None)) for _, starts, groups, _ in parts)
    steps = sorted({step for _, _, _, step in parts})
    operands = [factor.reshape(factor.shape[0], -1, step, size, size) for step in steps]

    def kernel(scal, pat, *refs):
        factor_refs = dict(zip(steps, refs))
        out_refs = refs[len(steps) + len(after) : -1]
        sems = refs[-1]
        copies = []
        for (rows, starts, groups, step), out_ref in zip(parts, out_refs):
            run = rows // len(starts(scal))
            part_copies = []
            for g, column in enumerate(groups(scal)):
                for n, start in enumerate(starts(scal)):
                    place = sum(map(len, copies)) + len(part_copies)
                    part_copies.append(
                        pltpu.make_async_copy(
                            factor_refs[step].at[
                                pl.ds(start, run), pl.ds(column // step, 2), column % step
                            ],
                            out_ref.at[g, pl.ds(n * run, run)],
                            sems.at[place],
                        )
                    )
            for copy in part_copies:
                copy.start()
            copies.append(part_copies)
        for (rows, starts, groups, step), out_ref, part_copies in zip(parts, out_refs, copies):
            first_rows = starts(scal)
            run = rows // len(first_rows)
            for g, column in enumerate(groups(scal)):
                for n, start in enumerate(first_rows):
                    part_copies[g * len(first_rows) + n].wait()
                    for i in range(run):
                        for k in range(2):

                            @pl.when(pat[start + i, column + k * step] == 0)
                            def _(g=g, n=n, i=i, k=k, run=run, out_ref=out_ref):
                                out_ref[g, n * run + i, k] = jnp.zeros((size, size), jnp.bfloat16)

    return pl.pallas_call(
        kernel,
        grid_spec=pltpu.PrefetchScalarGridSpec(
            num_scalar_prefetch=2,
            grid=(1,),
            in_specs=[pl.BlockSpec(memory_space=pl.ANY)] * (len(steps) + len(after)),
            out_specs=[pl.BlockSpec(memory_space=pltpu.VMEM)] * len(parts),
            scratch_shapes=[pltpu.SemaphoreType.DMA((copy_count,))],
        ),
        out_shape=[jax.ShapeDtypeStruct(shape, jnp.bfloat16) for shape in shapes],
        compiler_params=params(),
        cost_estimate=pl.CostEstimate(
            flops=0, bytes_accessed=sum(8 * math.prod(shape) for shape in shapes), transcendentals=0
        ),
        name="lay_out",
    )(scalars, pltpu.with_memory_space_constraint(pattern, pltpu.HBM), *[pltpu.with_memory_space_constraint(operand, pltpu.HBM) for operand in operands], *after)


def block_sums(parts, first_row, row_count, acc, base, negate):
    size, rhs = parts[0][1][0].shape[1:]
    rows = slice(first_row, first_row + row_count)

    def kernel(*refs):
        refs = list(refs)
        out_ref = refs.pop()
        total = jnp.zeros((row_count * size, rhs), jnp.float32)
        for blocks, values in parts:
            blocks_ref = refs.pop(0)
            place = 0
            for value in values:
                value_ref = refs.pop(0)
                for start in range(0, value.shape[0], 2):
                    right = value_ref[start : start + 2].reshape(2 * size, rhs)
                    left = jnp.concatenate([blocks_ref[place, rows, n] for n in range(2)], axis=2)
                    left = left.reshape(row_count * size, 2 * size)
                    total = total + jnp.dot(left, right, preferred_element_type=jnp.float32)
                    place += 1
        total = total.reshape(row_count, size, rhs)
        if acc is not None:
            total = total + refs.pop(0)[acc[1] : acc[1] + row_count]
        if base is not None:
            total = total - refs.pop(0)[base[1] : base[1] + row_count].astype(jnp.float32)
        out_ref[...] = (-total if negate else total).astype(out_ref.dtype)

    operands = []
    for blocks, values in parts:
        operands += [blocks, *values]
    operands += [extra[0] for extra in (acc, base) if extra is not None]
    blocks_used = 2 * row_count * sum(blocks.shape[0] for blocks, _ in parts)
    return pl.pallas_call(
        kernel,
        out_shape=jax.ShapeDtypeStruct((row_count, size, rhs), jnp.bfloat16 if negate else jnp.float32),
        compiler_params=params(),
        cost_estimate=pl.CostEstimate(
            flops=2 * blocks_used * size * size * rhs, bytes_accessed=2 * blocks_used * size * size, transcendentals=0
        ),
        name="block_sums",
    )(*operands)


def low_sums(blocks, values, acc, chunks):
    rows, size, rhs = acc.shape

    def kernel(blocks_ref, *refs):
        value_refs, acc_ref, out_refs = refs[: len(values)], refs[len(values)], refs[len(values) + 1 :]
        total = acc_ref[...].reshape(rows * size, rhs)
        place = 0
        for value, ref in zip(values, value_refs):
            for start in range(0, value.shape[0], 2):
                left = jnp.concatenate([blocks_ref[place, :, n] for n in range(2)], axis=2)
                right = ref[start : start + 2].reshape(2 * size, rhs)
                total = total + jnp.dot(
                    left.reshape(rows * size, 2 * size), right, preferred_element_type=jnp.float32
                )
                place += 1
        total = (-total).astype(jnp.bfloat16).reshape(chunks, rows // chunks, size, rhs)
        for n, ref in enumerate(out_refs):
            ref[...] = total[n]

    return pl.pallas_call(
        kernel,
        out_shape=[jax.ShapeDtypeStruct((rows // chunks, size, rhs), jnp.bfloat16)] * chunks,
        compiler_params=params(),
        name="low_sums",
    )(blocks, *values, acc)


def sum_and_solve(terms, inverses, row_start):
    rows, size, rhs = terms[0].shape
    term_count = len(terms)

    def kernel(*refs):
        term_refs = refs[:term_count]
        inverse_refs = refs[term_count:-1]
        for i in range(rows):
            value = term_refs[0][i].astype(jnp.float32)
            for ref in term_refs[1:]:
                value = value + ref[i].astype(jnp.float32)
            value = value.astype(jnp.bfloat16)
            for inverse_ref in inverse_refs:
                value = jnp.dot(inverse_ref[i, 0], value, preferred_element_type=jnp.float32).astype(jnp.bfloat16)
            refs[-1][i] = value

    whole = pl.BlockSpec((rows, size, rhs), lambda g: (0, 0, 0))
    inverse = pl.BlockSpec((rows, 1, size, size), lambda g: (row_start // rows, 0, 0, 0))
    return pl.pallas_call(
        kernel,
        grid=(1,),
        in_specs=[whole] * term_count + [inverse] * len(inverses),
        out_specs=whole,
        out_shape=jax.ShapeDtypeStruct((rows, size, rhs), jnp.bfloat16),
        compiler_params=params(),
        cost_estimate=pl.CostEstimate(
            flops=2 * rows * size * size * rhs, bytes_accessed=2 * (term_count + 2) * rows * size * rhs, transcendentals=0
        ),
        name="sum_and_solve",
    )(*terms, *inverses)


def solve_blocks(inverse, values, after):
    count, size, rhs = values.shape

    def kernel(inverse_ref, value_ref, *refs):
        out_ref = refs[-1]
        for i in range(count):
            out_ref[i] = jnp.dot(inverse_ref[i], value_ref[i], preferred_element_type=jnp.float32).astype(jnp.bfloat16)

    return pl.pallas_call(
        kernel,
        in_specs=[pl.BlockSpec(memory_space=pltpu.VMEM)] * 2 + [pl.BlockSpec(memory_space=pl.ANY)] * len(after),
        out_shape=jax.ShapeDtypeStruct(values.shape, jnp.bfloat16),
        compiler_params=params(),
        name="solve_blocks",
    )(inverse, values, *after)


def low_base(scalars, zero, keep, per, q_n, lo_n):
    chunks, size, rhs = zero[0].shape
    scalars = jnp.concatenate([scalars, keep[None].astype(jnp.int32)])

    def kernel(scal, *refs):
        out_ref = refs[-1]
        for h in range(per):
            source = scal[1] ^ (h * q_n + scal[0])
            for r in range(chunks):
                value = jnp.zeros((size, rhs), jnp.bfloat16)
                for t, ref in enumerate(refs[:-1]):
                    value = jnp.where((source == t) & (scal[3] > 0), ref[r], value)
                place = lax.rem(r + lo_n - scal[2], lo_n)
                out_ref[place * per + h] = value

    return pl.pallas_call(
        kernel,
        grid_spec=pltpu.PrefetchScalarGridSpec(
            num_scalar_prefetch=1,
            grid=(1,),
            in_specs=[pl.BlockSpec(memory_space=pltpu.VMEM)] * len(zero),
            out_specs=pl.BlockSpec(memory_space=pltpu.VMEM),
        ),
        out_shape=jax.ShapeDtypeStruct((chunks * per, size, rhs), jnp.bfloat16),
        compiler_params=params(),
        name="low_base",
    )(scalars, *zero)


def last_solve(own, other, inverse, solved, copies):
    count, size, rhs = own.shape

    def kernel(own_ref, other_ref, inverse_ref, solved_ref, out_ref):
        for h in range(count):
            value = (own_ref[h] + other_ref[h].astype(jnp.float32)).astype(jnp.bfloat16)
            value = jnp.dot(inverse_ref[h, 0], value, preferred_element_type=jnp.float32)
            value = (value + solved_ref[h].astype(jnp.float32)).astype(jnp.bfloat16)
            for copy in range(copies):
                out_ref[h * copies + copy] = value

    return pl.pallas_call(
        kernel,
        out_shape=jax.ShapeDtypeStruct((count * copies, size, rhs), jnp.bfloat16),
        compiler_params=params(),
        name="last_solve",
    )(own, other, inverse, solved)


def on_device(right_sides, factor, pattern, lower_inverse, upper_inverse):
    lo_n = lax.axis_size("lo")
    prow_n = lax.axis_size("hi") * lo_n
    q_n = lax.axis_size("q")
    pcol_n = q_n * lax.axis_size("s")
    row_id = lax.axis_index("hi") * lo_n + lax.axis_index("lo")
    q_id = lax.axis_index("q")
    s_id = lax.axis_index("s")
    col_id = q_id * prow_n + s_id
    row_blocks, _, col_blocks, _, size, _ = factor.shape
    rhs = right_sides.shape[1]
    per = right_sides.shape[0] // size
    spread_n = pcol_n // per
    half = row_blocks // 2
    bounds = (0, half, 3 * row_blocks // 4, 7 * row_blocks // 8, row_blocks)
    cols = tuple(q_n * b for b in bounds)
    device = lambda r, c: r * pcol_n + c
    everyone = [(r, c) for r in range(prow_n) for c in range(pcol_n)]

    is_low = row_id < prow_n // 2
    hi_id = lax.axis_index("hi")
    lo_id = lax.axis_index("lo")
    entries = [q_id, col_id, lo_id]
    scalars = jnp.stack([jnp.asarray(v, jnp.int32) for v in entries])
    pattern = pattern.reshape(row_blocks, col_blocks)
    first_low = half // per

    def route(t, r, c):
        q, s = divmod(c, prow_n)
        up, low = divmod(r, lo_n)
        if t == 0:
            return s, q * prow_n + (1 - up) * lo_n + low
        up = (up + 1 + s // lo_n + q) % 2
        return s, (q + t) % q_n * prow_n + up * lo_n + lo_n - 1 - low

    def spread(values):
        return [
            lax.ppermute(values, ALL_AXES, [(device(r, c), device(*route(t, r, c))) for r, c in everyone])
            for t in reversed(range(q_n))
        ][::-1]

    def spread_groups(first, last):
        def groups(scal):
            ids = [lax.rem(scal[0] + (q_n - t), q_n) if scal is not None else 0 for t in range(q_n)]
            return [q_n * m + q for q in ids for m in range(first, last, 2)]

        return groups

    def summands(partial):
        step = prow_n // 2
        while True:
            pairs = [(device(r, c), device(r ^ step, c)) for r, c in everyone]
            other = lax.ppermute(partial, ALL_AXES, pairs)
            step //= 2
            if step == 0:
                return [partial, other]
            partial = partial + other

    def count(level):
        return bounds[level + 1] - bounds[level]

    def part(level, groups, step):
        return (count(level), lambda scal: [bounds[level]], groups, step)

    def laid_out(after, *parts):
        return lay_out(scalars, pattern, factor, after, parts)

    low_starts = lambda scal: [per * lax.rem(scal[2] + t, lo_n) if scal is not None else 0 for t in range(lo_n)]
    low_rows = (half, low_starts)
    late_rows = (count(2) + count(3), lambda scal: [bounds[2]])

    if per == prow_n and lo_n == 2 and pcol_n & (pcol_n - 1) == 0:

        def chunk(r, c):
            q, s = c // prow_n, c % prow_n
            return (r // lo_n + s // lo_n + 1 + q) % 2 * lo_n + r % lo_n

        there = [(device(r, c), device(c % prow_n, chunk(r, c) * q_n + c // prow_n)) for r, c in everyone]
        back = [(target, source) for source, target in there]
        chunk_id = chunk(row_id, col_id)
        inverse_rows = lax.dynamic_index_in_dim(
            lower_inverse[:half].reshape(first_low, per, size, size), chunk_id, 1, keepdims=False
        )

        def zero_groups(scal):
            ids = [scal[1] ^ t if scal is not None else 0 for t in range(pcol_n)]
            return [c + pcol_n * r for c in ids for r in range(0, first_low, 2)]

        def exchange(values, t):
            return lax.ppermute(values, ALL_AXES, [(device(r, c), device(r, c ^ t)) for r, c in everyone])

        (one_zero,) = laid_out([inverse_rows], part(1, zero_groups, pcol_n))
        inverse_rows = lax.ppermute(inverse_rows, ALL_AXES, there)
        blocks = right_sides.reshape(2, 2, size, rhs)
        for axis, name, index in ((0, "hi", hi_id), (1, "lo", lo_id)):
            other = lax.dynamic_index_in_dim(blocks, 1 - index, axis, keepdims=False)
            other = lax.ppermute(other, name, [(0, 1), (1, 0)])
            own = lax.dynamic_index_in_dim(blocks, index, axis, keepdims=False)
            blocks = jnp.where(index == 0, jnp.stack([own, other], axis), jnp.stack([other, own], axis))
        blocks = blocks.reshape(per, size, rhs)
        own_zero = solve_blocks(inverse_rows, blocks[:first_low], [one_zero])
        even = {t: exchange(own_zero, t) for t in range(pcol_n - 2, 0, -2)}
        even[0] = own_zero
        zero = []
        for t in range(0, pcol_n, 2):
            zero += [even[t], exchange(even[t], 1)]
        rest = lax.ppermute(blocks[first_low:], ALL_AXES, back)
        zero_step = pcol_n

        owned = (jnp.arange(per) == chunk_id)[None, :, None, None]
        base = jnp.where(owned, rest[:, None], jnp.zeros((), jnp.bfloat16)).reshape(row_blocks - half, size, rhs)
        base_zero = low_base(scalars, zero, row_id == s_id, per, q_n, lo_n)
    else:
        group_rows = lax.all_gather(right_sides.reshape(per, size, rhs), COL_AXES, axis=0, tiled=True)
        picked = lax.dynamic_index_in_dim(group_rows.reshape(per, pcol_n, size, rhs), col_id, 1, keepdims=False)
        mine = lax.all_gather(picked, ROW_AXES, axis=0, tiled=True)
        own_zero = sum_and_solve([mine[:half]], [lower_inverse], 0)
        zero_groups = spread_groups(0, half)
        zero_step = q_n
        (one_zero,) = laid_out([own_zero], part(1, zero_groups, zero_step))
        zero = spread(own_zero)
        base = jnp.where(row_id == 0, mine[half:], jnp.zeros((), jnp.bfloat16))
        base_zero = jnp.where(row_id == 0, own_zero, jnp.zeros((), jnp.bfloat16))
        base_zero = lax.dynamic_slice_in_dim(jnp.concatenate([base_zero, base_zero]), per * lo_id, half, 0)

    level_groups = [zero_groups] + [spread_groups(bounds[level], bounds[level + 1]) for level in range(1, 4)]
    partial = block_sums([(one_zero, zero)], 0, count(1), None, (base, 0), True)
    one_rows = sum_and_solve(summands(partial), [lower_inverse], bounds[1])
    one = spread(one_rows)
    late_zero, two_one = laid_out([one_rows, base_zero], (*late_rows, zero_groups, zero_step), part(2, level_groups[1], q_n))
    late = block_sums([(late_zero, zero)], 0, count(2) + count(3), None, (base, bounds[2] - half), False)
    partial = block_sums([(two_one, one)], 0, count(2), (late, 0), None, True)
    two_rows = sum_and_solve(summands(partial), [lower_inverse], bounds[2])
    two = spread(two_rows)
    three_one, three_two = laid_out([two_rows], part(3, level_groups[1], q_n), part(3, level_groups[2], q_n))
    late = block_sums([(three_one, one)], 0, count(3), (late, count(2)), None, False)
    partial = block_sums([(three_two, two)], 0, count(3), (late, 0), None, True)
    three_solved = sum_and_solve(summands(partial), [lower_inverse, upper_inverse], bounds[3])
    three = spread(three_solved)
    two_three, one_three, one_two, zero_three = laid_out(
        [three_solved],
        part(2, level_groups[3], q_n),
        part(1, level_groups[3], q_n),
        part(1, level_groups[2], q_n),
        (*low_rows, level_groups[3], q_n),
    )
    partial = block_sums([(two_three, three)], 0, count(2), None, None, True)
    two_solved = sum_and_solve(summands(partial) + [two_rows], [upper_inverse], bounds[2])
    two = spread(two_solved)
    zero_two, zero_one = laid_out([two_solved], (*low_rows, level_groups[2], q_n), (*low_rows, level_groups[1], q_n))
    late = block_sums([(one_three, three)], 0, count(1), None, None, False)
    partial = block_sums([(one_two, two)], 0, count(1), (late, 0), None, True)
    one_solved = sum_and_solve(summands(partial) + [one_rows], [upper_inverse], bounds[1])
    one = spread(one_solved)
    upper = block_sums([(zero_three, three), (zero_two, two)], 0, half, None, (base_zero, 0), False)
    own, *chunks = low_sums(zero_one, one, upper, lo_n)
    own = own.astype(jnp.float32)
    for t in range(1, lo_n):
        pairs = [((lo, (lo + t) % lo_n)) for lo in range(lo_n)]
        own = own + lax.ppermute(chunks[t - 1], "lo", pairs).astype(jnp.float32)
    other = lax.ppermute(own.astype(jnp.bfloat16), "hi", [(0, 1), (1, 0)])
    solved = jnp.concatenate([one_solved, two_solved, three_solved], axis=0)
    solved = lax.dynamic_slice_in_dim(solved, per * lo_id, per, 0)
    last_inverse = lax.dynamic_slice_in_dim(upper_inverse, per * lo_id, per, 0)
    last_inverse = jnp.where(is_low, last_inverse, jnp.zeros((), jnp.bfloat16))
    solved = jnp.where(is_low, jnp.zeros((), jnp.bfloat16), solved)
    if spread_n == 2 and per & (per - 1) == 0:
        upper_id, last_id = col_id // 2, col_id % 2
        rows = last_solve(own, other, last_inverse, solved, 1)

        def pick(blocks, index):
            return lax.dynamic_index_in_dim(blocks, index, 0, keepdims=False)

        def crossed(values, t):
            return lax.ppermute(values, ALL_AXES, [(device(r, c), device(r, c ^ t)) for r, c in everyone])

        received = [crossed(pick(rows, upper_id ^ t), 2 * t) for t in range(1, per)]
        received = jnp.stack([pick(rows, upper_id)] + received)
        kept, sent = [
            jnp.stack([pick(received, upper_id ^ (per // 2 * p + i)) for i in range(per // 2)])
            for p in (last_id, 1 - last_id)
        ]
        sent = crossed(sent, 1)
        mine = jnp.where(last_id == 0, jnp.stack([kept, sent], 1), jnp.stack([sent, kept], 1))
    else:
        slots = last_solve(own, other, last_inverse, solved, spread_n)
        received = lax.all_to_all(slots, COL_AXES, 0, 0, tiled=True)
        mine = lax.dynamic_slice_in_dim(received, lax.rem(col_id, spread_n) * per, per, 0)
    return mine.reshape(per * size, rhs)


def solution(mesh):
    prow_n, pcol_n = mesh.shape["prow"], mesh.shape["pcol"]
    fine = Mesh(mesh.devices.reshape(2, prow_n // 2, pcol_n // prow_n, prow_n), ALL_AXES)
    placed = (
        P(ALL_AXES, None),
        P(None, COL_AXES, None, ROW_AXES, None, None),
        P(None, COL_AXES, None, ROW_AXES),
        P(None, COL_AXES, None, None),
        P(None, COL_AXES, None, None),
    )
    return jax.shard_map(on_device, mesh=fine, in_specs=placed, out_specs=P(ALL_AXES, None), check_vma=False)
```
